32 devices in a mesh: band: 4 (over y, core), grid: 8 (over z, x).
Axes of the slice: x: 2, y: 2, z: 4, core: 2. Of those that a mesh axis runs over, the one named last changes fastest.
Arguments:
- bands: float32 [4, 2, 128, 128, 128], P('band', None, 'grid'), may hold values from -6 to 6
- coulomb: float32 [128, 128, 128], P(None, 'grid'), may hold values from 0.1 to 10
Outputs:
- exchange: float32 [4, 2, 128, 128, 128], P('band', None, 'grid')
The draws below stay inside these ranges and needn't reach their ends.
All inputs are finite; a program needn't handle non-finite values.
Results may differ from the reference program's by a relative error of at most 0.0001.
Values sent between devices are 32-bit elements; how exact they have to be, the bound alone decides.
A program may use at most 64 MiB of HBM per device.

```python
import math
import jax
import jax.numpy as jnp
from jax import lax

NX = 128
NY = 128
NZ = 128
LOCAL = 1
STEPS = 2
BANDS = 4
N_BAND = 4


def block_levels(rng, extent, shards, least, largest):
    def one(dim, shards_of):
        steps = jax.random.uniform(jax.random.fold_in(jax.random.fold_in(rng, 6), dim), (shards_of,), jnp.float32, least / len(shards), largest / len(shards))
        return jnp.repeat(jnp.exp(steps), extent[dim] // shards_of).reshape((-1,) + (1,) * (len(extent) - dim - 1))

    factor_of = one(*shards[0])
    for cut in shards[1:]:
        factor_of = factor_of * one(*cut)
    return factor_of


def noise(key, dims, scale, reach, split=(), dtype=jnp.bfloat16):
    gain = block_levels(key, dims, split, -0.22, 0.18) if split else 1.0
    values = jax.random.normal(key, dims, jnp.float32) * scale * gain
    return jnp.minimum(jnp.maximum(values, -reach), reach).astype(dtype)


def setup_inputs(seed: int = 0) -> dict:
    key_of = jax.random.split(jax.random.key(seed), 3)
    bands = noise(key_of[0], (BANDS, 2, NX, NY, NZ), 0.7, 6.0, ((0, 4), (2, 8)), jnp.float32)
    coulomb = jnp.clip(jnp.exp(math.log(10.0) - 4.6051702 * jax.random.uniform(key_of[1], (NX, NY, NZ), jnp.float32) ** block_levels(key_of[1], (NX, NY, NZ), ((1, 8),), -0.2, 0.2)), 0.1, 10.0)
    return {"bands": bands, "coulomb": coulomb}


def reference(bands, coulomb):
    wave = lax.complex(bands[:, 0], bands[:, 1])
    pieces = []
    for step_index in range(STEPS):
        owner = (step_index * N_BAND) // STEPS
        pieces.append(wave[owner * LOCAL:(owner + 1) * LOCAL])
    visitors = jnp.concatenate(pieces, axis=0)

    def one_band(orbital):
        total = jnp.zeros_like(orbital)
        for visit_index in range(STEPS * LOCAL):
            partner = visitors[visit_index]
            density = jnp.conj(partner) * orbital
            potential = jnp.fft.ifftn(coulomb * jnp.fft.fftn(density))
            total = total + partner * potential
        return -0.25 * total

    result = lax.map(one_band, wave)
    return jnp.stack([result.real, result.imag], axis=1).astype(jnp.float32)
```

```python
import functools

import jax
import jax.numpy as jnp
import ml_dtypes
import numpy as np
from jax import lax
from jax.experimental import pallas as pl
from jax.experimental.pallas import tpu as pltpu
from jax.sharding import PartitionSpec as P

STEPS = 2
VMEM_LIMIT = 48 * 1024 * 1024


def split_table(table):
    high = table.astype(ml_dtypes.bfloat16)
    low = (table - high.astype(np.float64)).astype(ml_dtypes.bfloat16)
    return np.stack([high, low])


def tables(length, scale):
    index = np.arange(length)
    angle = (index[:, None] * index[None, :] % length) * (2.0 * np.pi / length)
    cosine, sine = np.cos(angle), np.sin(angle)
    forward = np.block([[cosine, sine], [-sine, cosine]])
    inverse = np.block([[cosine, -sine], [sine, cosine]])
    return [split_table(t) for t in (forward, inverse, inverse * scale, forward.T, inverse.T)]


def split(values):
    high = values.astype(jnp.bfloat16)
    return high, (values - high.astype(jnp.float32)).astype(jnp.bfloat16)


def dot(a, b):
    return jnp.dot(a, b, preferred_element_type=jnp.float32)


def left(table_ref, values):
    high, low = split(values)
    return dot(table_ref[0], high) + (dot(table_ref[1], high) + dot(table_ref[0], low))


def right(values, table_ref):
    high, low = split(values)
    return dot(high, table_ref[0]) + (dot(high, table_ref[1]) + dot(low, table_ref[0]))


def forward_kernel(own_ref, vis_ref, left_ref, right_ref, out_ref):
    planes, ny, nz = own_ref.shape[2:]
    shards, _, rows = out_ref.shape[:3]
    own_re, own_im, vis_re, vis_im = own_ref[0, 0], own_ref[0, 1], vis_ref[0, 0], vis_ref[0, 1]
    real = vis_re * own_re + vis_im * own_im
    imag = vis_re * own_im - vis_im * own_re
    pair = jnp.concatenate([real.reshape(planes * ny, nz), imag.reshape(planes * ny, nz)], axis=1)
    lines = right(pair, right_ref)
    for i in range(0, planes, 2):
        both = [
            jnp.concatenate([lines[p * ny:(p + 1) * ny, :nz], lines[p * ny:(p + 1) * ny, nz:]], axis=0)
            for p in (i, i + 1)
        ]
        result = left(left_ref, jnp.concatenate(both, axis=1))
        for p in range(2):
            for part in range(2):
                piece = result[part * ny:(part + 1) * ny, p * nz:(p + 1) * nz]
                out_ref[:, part, :, i + p, :] = piece.reshape(shards, rows, nz)


def pencil_kernel(in_ref, coulomb_ref, forward_ref, inverse_ref, out_ref):
    shards, _, rows, planes, nz = in_ref.shape
    nx = shards * planes
    for k in range(0, rows, 2):
        both = []
        for q in (k, k + 1):
            both.append(
                jnp.concatenate([in_ref[:, part, q].reshape(nx, nz) for part in range(2)], axis=0)
            )
        weight = jnp.concatenate([coulomb_ref[:, k, :], coulomb_ref[:, k + 1, :]], axis=1)
        value = left(forward_ref, jnp.concatenate(both, axis=1))
        value = value * jnp.concatenate([weight, weight], axis=0)
        value = left(inverse_ref, value)
        for q in range(2):
            for part in range(2):
                piece = value[part * nx:(part + 1) * nx, q * nz:(q + 1) * nz]
                out_ref[:, part, k + q] = piece.reshape(shards, planes, nz)


def inverse_kernel(has_base, in_ref, vis_ref, left_ref, right_ref, *rest):
    base_ref, out_ref = rest if has_base else (None, rest[0])
    shards, _, rows, planes, nz = in_ref.shape
    ny = shards * rows
    for i in range(0, planes, 2):
        both = []
        for p in (i, i + 1):
            both.append(
                jnp.concatenate([in_ref[:, part, :, p, :].reshape(ny, nz) for part in range(2)], axis=0)
            )
        result = left(left_ref, jnp.concatenate(both, axis=1))
        for p in range(2):
            cut = result[:, p * nz:(p + 1) * nz]
            value = right(jnp.concatenate([cut[:ny], cut[ny:]], axis=1), right_ref)
            pot_re, pot_im = -0.25 * value[:, :nz], -0.25 * value[:, nz:]
            vis_re, vis_im = vis_ref[0, 0, i + p], vis_ref[0, 1, i + p]
            out_re = pot_re * vis_re - pot_im * vis_im
            out_im = pot_re * vis_im + pot_im * vis_re
            if has_base:
                out_re = out_re + base_ref[0, 0, i + p]
                out_im = out_im + base_ref[0, 1, i + p]
            out_ref[0, 0, i + p] = out_re
            out_ref[0, 1, i + p] = out_im


def whole_spec(array):
    return pl.BlockSpec(array.shape, lambda i: (0,) * array.ndim)


def forward(own, vis, shards, tabs):
    _, _, planes, ny, nz = own.shape
    step = min(8, planes)
    slab = pl.BlockSpec((1, 2, step, ny, nz), lambda i: (0, 0, i, 0, 0))
    return pl.pallas_call(
        forward_kernel,
        grid=(planes // step,),
        in_specs=[slab, slab, whole_spec(tabs[0]), whole_spec(tabs[3])],
        out_specs=pl.BlockSpec((shards, 2, ny // shards, step, nz), lambda i: (0, 0, 0, i, 0)),
        out_shape=jax.ShapeDtypeStruct((shards, 2, ny // shards, planes, nz), jnp.float32),
        compiler_params=pltpu.CompilerParams(vmem_limit_bytes=VMEM_LIMIT),
        name="pair_density_dft",
    )(own, vis, tabs[0], tabs[3])


def pencil(block, coulomb, tabs):
    shards, _, rows, planes, nz = block.shape
    step = min(8, rows)
    spec = pl.BlockSpec((shards, 2, step, planes, nz), lambda i: (0, 0, i, 0, 0))
    return pl.pallas_call(
        pencil_kernel,
        grid=(rows // step,),
        in_specs=[
            spec,
            pl.BlockSpec((coulomb.shape[0], step, nz), lambda i: (0, i, 0)),
            whole_spec(tabs[0]),
            whole_spec(tabs[2]),
        ],
        out_specs=spec,
        out_shape=jax.ShapeDtypeStruct(block.shape, jnp.float32),
        compiler_params=pltpu.CompilerParams(vmem_limit_bytes=VMEM_LIMIT),
        name="screen_pencils",
    )(block, coulomb, tabs[0], tabs[2])


def inverse(block, vis, base, tabs):
    shards, _, rows, planes, nz = block.shape
    step = min(8, planes)
    slab = pl.BlockSpec((1, 2, step, shards * rows, nz), lambda i: (0, 0, i, 0, 0))
    extra = [] if base is None else [base]
    return pl.pallas_call(
        functools.partial(inverse_kernel, base is not None),
        grid=(planes // step,),
        in_specs=[
            pl.BlockSpec((shards, 2, rows, step, nz), lambda i: (0, 0, 0, i, 0)),
            slab,
            whole_spec(tabs[1]),
            whole_spec(tabs[4]),
        ] + [slab] * len(extra),
        out_specs=slab,
        out_shape=jax.ShapeDtypeStruct(vis.shape, jnp.float32),
        compiler_params=pltpu.CompilerParams(vmem_limit_bytes=VMEM_LIMIT),
        name="potential_to_exchange",
    )(block, vis, tabs[1], tabs[4], *extra)


def body(bands, coulomb):
    groups = lax.axis_size("band")
    shards = lax.axis_size("grid")
    span = groups // STEPS
    nx, ny, nz = coulomb.shape[0], bands.shape[3], bands.shape[4]
    tabs = [jnp.asarray(t) for t in tables(nx, 1.0 / (nx * ny * nz))]

    place = lax.axis_index("band") % span
    near = bands
    reach = 1
    while reach < span:
        moves = [(s * span + i, s * span + i + reach) for s in range(STEPS) for i in range(min(reach, span - reach))]
        arrived = lax.ppermute(near, "band", moves)
        near = jnp.where((place >= reach) & (place < 2 * reach), arrived, near)
        reach *= 2
    visitors = [near]
    for _ in range(STEPS - 1):
        visitors.append(lax.ppermute(visitors[-1], "band", [(i, (i + span) % groups) for i in range(groups)]))

    total = None
    sent = [forward(bands, vis, shards, tabs) for vis in visitors]
    sent = [lax.all_to_all(s, "grid", 0, 0, tiled=True) for s in sent]
    sent = [pencil(s, coulomb, tabs) for s in sent]
    sent = [lax.all_to_all(s, "grid", 0, 0, tiled=True) for s in sent]
    for block, vis in zip(sent, visitors):
        total = inverse(block, vis, total, tabs)
    return total


def solution(mesh):
    in_specs = (P("band", None, "grid", None, None), P(None, "grid", None))
    out_specs = P("band", None, "grid", None, None)
    return jax.shard_map(body, mesh=mesh, in_specs=in_specs, out_specs=out_specs, check_vma=False)
```

```python
import functools

import jax
import jax.numpy as jnp
import ml_dtypes
import numpy as np
from jax import lax
from jax.experimental import pallas as pl
from jax.experimental.pallas import tpu as pltpu
from jax.sharding import PartitionSpec as P

STEPS = 2
VMEM_LIMIT = 48 * 1024 * 1024


def split_table(table):
    high = table.astype(ml_dtypes.bfloat16)
    low = (table - high.astype(np.float64)).astype(ml_dtypes.bfloat16)
    return np.stack([high, low])


def tables(length, scale):
    index = np.arange(length)
    angle = (index[:, None] * index[None, :] % length) * (2.0 * np.pi / length)
    cosine, sine = np.cos(angle), np.sin(angle)
    forward = np.block([[cosine, sine], [-sine, cosine]])
    inverse = np.block([[cosine, -sine], [sine, cosine]])
    return [split_table(t) for t in (forward, inverse, inverse * scale, forward.T, inverse.T)]


def split(values):
    high = values.astype(jnp.bfloat16)
    return high, (values - high.astype(jnp.float32)).astype(jnp.bfloat16)


def dot(a, b):
    return jnp.dot(a, b, preferred_element_type=jnp.float32)


def left(table_ref, values):
    high, low = split(values)
    return dot(table_ref[0], high) + (dot(table_ref[1], high) + dot(table_ref[0], low))


def right(values, table_ref):
    high, low = split(values)
    return dot(high, table_ref[0]) + (dot(high, table_ref[1]) + dot(low, table_ref[0]))


def forward_kernel(own_ref, vis_ref, left_ref, right_ref, out_ref):
    planes, ny, nz = own_ref.shape[2:]
    shards, _, rows = out_ref.shape[:3]
    own_re, own_im, vis_re, vis_im = own_ref[0, 0], own_ref[0, 1], vis_ref[0, 0], vis_ref[0, 1]
    real = vis_re * own_re + vis_im * own_im
    imag = vis_re * own_im - vis_im * own_re
    pair = jnp.concatenate([real.reshape(planes * ny, nz), imag.reshape(planes * ny, nz)], axis=1)
    lines = right(pair, right_ref)
    for i in range(0, planes, 2):
        both = [
            jnp.concatenate([lines[p * ny:(p + 1) * ny, :nz], lines[p * ny:(p + 1) * ny, nz:]], axis=0)
            for p in (i, i + 1)
        ]
        result = left(left_ref, jnp.concatenate(both, axis=1))
        for p in range(2):
            for part in range(2):
                piece = result[part * ny:(part + 1) * ny, p * nz:(p + 1) * nz]
                out_ref[:, part, :, i + p, :] = piece.reshape(shards, rows, nz)


def pencil_kernel(in_ref, coulomb_ref, forward_ref, inverse_ref, out_ref):
    shards, _, rows, planes, nz = in_ref.shape
    nx = shards * planes
    for k in range(0, rows, 2):
        both = []
        for q in (k, k + 1):
            both.append(
                jnp.concatenate([in_ref[:, part, q].reshape(nx, nz) for part in range(2)], axis=0)
            )
        weight = jnp.concatenate([coulomb_ref[:, k, :], coulomb_ref[:, k + 1, :]], axis=1)
        value = left(forward_ref, jnp.concatenate(both, axis=1))
        value = value * jnp.concatenate([weight, weight], axis=0)
        value = left(inverse_ref, value)
        for q in range(2):
            for part in range(2):
                piece = value[part * nx:(part + 1) * nx, q * nz:(q + 1) * nz]
                out_ref[:, part, k + q] = piece.reshape(shards, planes, nz)


def inverse_kernel(has_base, in_ref, vis_ref, left_ref, right_ref, *rest):
    base_ref, out_ref = rest if has_base else (None, rest[0])
    shards, _, rows, planes, nz = in_ref.shape
    ny = shards * rows
    for i in range(0, planes, 2):
        both = []
        for p in (i, i + 1):
            both.append(
                jnp.concatenate([in_ref[:, part, :, p, :].reshape(ny, nz) for part in range(2)], axis=0)
            )
        result = left(left_ref, jnp.concatenate(both, axis=1))
        for p in range(2):
            cut = result[:, p * nz:(p + 1) * nz]
            value = right(jnp.concatenate([cut[:ny], cut[ny:]], axis=1), right_ref)
            pot_re, pot_im = -0.25 * value[:, :nz], -0.25 * value[:, nz:]
            vis_re, vis_im = vis_ref[0, 0, i + p], vis_ref[0, 1, i + p]
            out_re = pot_re * vis_re - pot_im * vis_im
            out_im = pot_re * vis_im + pot_im * vis_re
            if has_base:
                out_re = out_re + base_ref[0, 0, i + p]
                out_im = out_im + base_ref[0, 1, i + p]
            out_ref[0, 0, i + p] = out_re
            out_ref[0, 1, i + p] = out_im


def whole_spec(array):
    return pl.BlockSpec(array.shape, lambda i: (0,) * array.ndim)


def forward(own, vis, shards, tabs):
    _, _, planes, ny, nz = own.shape
    step = min(8, planes)
    slab = pl.BlockSpec((1, 2, step, ny, nz), lambda i: (0, 0, i, 0, 0))
    return pl.pallas_call(
        forward_kernel,
        grid=(planes // step,),
        in_specs=[slab, slab, whole_spec(tabs[0]), whole_spec(tabs[3])],
        out_specs=pl.BlockSpec((shards, 2, ny // shards, step, nz), lambda i: (0, 0, 0, i, 0)),
        out_shape=jax.ShapeDtypeStruct((shards, 2, ny // shards, planes, nz), jnp.float32),
        compiler_params=pltpu.CompilerParams(vmem_limit_bytes=VMEM_LIMIT),
        name="pair_density_dft",
    )(own, vis, tabs[0], tabs[3])


def pencil(block, coulomb, tabs):
    shards, _, rows, planes, nz = block.shape
    step = min(8, rows)
    spec = pl.BlockSpec((shards, 2, step, planes, nz), lambda i: (0, 0, i, 0, 0))
    return pl.pallas_call(
        pencil_kernel,
        grid=(rows // step,),
        in_specs=[
            spec,
            pl.BlockSpec((coulomb.shape[0], step, nz), lambda i: (0, i, 0)),
            whole_spec(tabs[0]),
            whole_spec(tabs[2]),
        ],
        out_specs=spec,
        out_shape=jax.ShapeDtypeStruct(block.shape, jnp.float32),
        compiler_params=pltpu.CompilerParams(vmem_limit_bytes=VMEM_LIMIT),
        name="screen_pencils",
    )(block, coulomb, tabs[0], tabs[2])


def inverse(block, vis, base, tabs):
    shards, _, rows, planes, nz = block.shape
    step = min(8, planes)
    slab = pl.BlockSpec((1, 2, step, shards * rows, nz), lambda i: (0, 0, i, 0, 0))
    extra = [] if base is None else [base]
    return pl.pallas_call(
        functools.partial(inverse_kernel, base is not None),
        grid=(planes // step,),
        in_specs=[
            pl.BlockSpec((shards, 2, rows, step, nz), lambda i: (0, 0, 0, i, 0)),
            slab,
            whole_spec(tabs[1]),
            whole_spec(tabs[4]),
        ] + [slab] * len(extra),
        out_specs=slab,
        out_shape=jax.ShapeDtypeStruct(vis.shape, jnp.float32),
        compiler_params=pltpu.CompilerParams(vmem_limit_bytes=VMEM_LIMIT),
        name="potential_to_exchange",
    )(block, vis, tabs[1], tabs[4], *extra)


def by_pairs(bands, coulomb):
    groups = lax.axis_size("band")
    shards = lax.axis_size("grid")
    span = groups // STEPS
    nx, ny, nz = coulomb.shape[0], bands.shape[3], bands.shape[4]
    tabs = [jnp.asarray(t) for t in tables(nx, 1.0 / (nx * ny * nz))]

    place = lax.axis_index("band") % span
    near = bands
    reach = 1
    while reach < span:
        moves = [(s * span + i, s * span + i + reach) for s in range(STEPS) for i in range(min(reach, span - reach))]
        arrived = lax.ppermute(near, "band", moves)
        near = jnp.where((place >= reach) & (place < 2 * reach), arrived, near)
        reach *= 2
    visitors = [near]
    for _ in range(STEPS - 1):
        visitors.append(lax.ppermute(visitors[-1], "band", [(i, (i + span) % groups) for i in range(groups)]))

    total = None
    sent = [forward(bands, vis, shards, tabs) for vis in visitors]
    sent = [lax.all_to_all(s, "grid", 0, 0, tiled=True) for s in sent]
    sent = [pencil(s, coulomb, tabs) for s in sent]
    sent = [lax.all_to_all(s, "grid", 0, 0, tiled=True) for s in sent]
    for block, vis in zip(sent, visitors):
        total = inverse(block, vis, total, tabs)
    return total


def permuted_tables(length, scale, row_order, plane_order):
    index = np.arange(length)
    angle = (index[:, None] * index[None, :] % length) * (2.0 * np.pi / length)
    cosine, sine = np.cos(angle), np.sin(angle)
    forward = np.block([[cosine, sine], [-sine, cosine]])
    inverse = np.block([[cosine, -sine], [sine, cosine]])
    rows = np.concatenate([row_order, row_order + length])
    planes = np.concatenate([plane_order, plane_order + length])
    return [
        split_table(t)
        for t in (
            forward.T,
            forward[rows],
            forward[:, planes],
            inverse[planes] * scale,
            inverse[:, rows],
            inverse.T,
        )
    ]


GROUPS = 4
HALVES = 2
PLANE_BAND = (0, 1, 3, 2)
PLANE_SLOT = (0, 2, 3, 1)


def fused_kernel(
    spread,
    bands_ref, coulomb_ref, zf_ref, yf_ref, xf_ref, xi_ref, yi_ref, zi_ref,
    out_ref,
    held, screen, packed, lines, back, result, slab,
    s1, r1, s2, r2, su, ru, sd, rd, s4, r4, s6, r6, s7, r7, s8, r8, loc,
):
    n = GROUPS
    peers = n * spread
    band = lax.axis_index("band")
    grid = lax.axis_index("grid")
    z = grid // spread
    t = grid % spread
    me = band * spread + t
    ny, nz = bands_ref.shape[3], bands_ref.shape[4]
    rows = ny // peers
    nx = peers * 2 * n * HALVES

    def remote(src, dst, send, recv, to_band, to_grid):
        return pltpu.make_async_remote_copy(
            src_ref=src, dst_ref=dst, send_sem=send, recv_sem=recv,
            device_id=(to_band, to_grid), device_id_type=pl.DeviceIdType.MESH,
        )

    def peer(k):
        q = (me + k) % peers
        return q, q // spread, z * spread + q % spread

    def line(k):
        return k * spread + t

    barrier = pltpu.get_barrier_semaphore()
    for k in range(1, peers):
        _, to_band, to_grid = peer(k)
        pl.semaphore_signal(barrier, inc=1, device_id=(to_band, to_grid), device_id_type=pl.DeviceIdType.MESH)
    for k in range(1, n):
        pl.semaphore_signal(
            barrier, inc=1, device_id=(band, line((z + k) % n)), device_id_type=pl.DeviceIdType.MESH
        )
    pl.semaphore_wait(barrier, peers - 1 + n - 1)

    slot = (band % 2) * 2 + band // 2

    def chunk(h, j):
        return bands_ref.at[0, :, pl.ds(j * n + h * 2, 2)]

    def first(h, d):
        to = (band + d) % n
        return remote(chunk(h, to), held.at[h, z, slot], s1.at[h, d], r1.at[h, d], to, grid)

    def first_local(h):
        return pltpu.make_async_copy(chunk(h, band), held.at[h, z, slot], loc.at[h])

    screen_local = pltpu.make_async_copy(coulomb_ref, screen.at[z], loc.at[HALVES])
    screen_local.start()
    for h in range(HALVES):
        first_local(h).start()
        for d in (2, 1, 3):
            first(h, d).start()

    def block(stream, src):
        return held.at[stream, src, pl.ds(0, 2)] if stream < HALVES else screen.at[src]

    def up(stream, d):
        return remote(
            block(stream, z - d), block(stream, z - d), su.at[stream, d], ru.at[stream, d], band, line(z + 1)
        )

    def down(stream, d):
        return remote(
            block(stream, z + d), block(stream, z + d), sd.at[stream, d], rd.at[stream, d], band, line(z - 1)
        )

    def hop(stream, d):
        if d > 0:
            @pl.when(z >= d)
            def _():
                pltpu.make_async_remote_copy(
                    src_ref=block(stream, z - d), dst_ref=block(stream, z - d),
                    send_sem=su.at[stream, d], recv_sem=ru.at[stream, d - 1],
                    device_id=(band, grid), device_id_type=pl.DeviceIdType.MESH,
                ).wait_recv()

            @pl.when(z + d < n)
            def _():
                pltpu.make_async_remote_copy(
                    src_ref=block(stream, z + d), dst_ref=block(stream, z + d),
                    send_sem=sd.at[stream, d], recv_sem=rd.at[stream, d - 1],
                    device_id=(band, grid), device_id_type=pl.DeviceIdType.MESH,
                ).wait_recv()
        if d < n - 1:
            @pl.when((z >= d) & (z + 1 < n))
            def _():
                up(stream, d).start()

            @pl.when((z + d < n) & (z >= 1))
            def _():
                down(stream, d).start()

    def hops_sent(stream):
        for d in range(n - 1):
            @pl.when((z >= d) & (z + 1 < n))
            def _():
                up(stream, d).wait_send()

            @pl.when((z + d < n) & (z >= 1))
            def _():
                down(stream, d).wait_send()

    def direct(h, c):
        to = c + 1
        part = held.at[h, z, 2 + c]
        return remote(part, part, s2.at[h, c], r2.at[h, z], band, line(to))

    for h in range(HALVES):
        first_local(h).wait()
        for d in range(1, n):
            first(h, d).wait_recv()
        hop(h, 0)
        for c in range(2):
            @pl.when(z != c + 1)
            def _():
                direct(h, c).start()
        if h == 0:
            hop(0, 1)
    screen_local.wait()
    hop(1, 1)
    hop(0, 2)
    hop(HALVES, 0)

    own = jnp.where(z == 0, 0, jnp.where(z == 1, 2, jnp.where(z == 2, 3, 1)))

    def received(h):
        for src in range(n):
            @pl.when((z != src) & ((z == 1) | (z == 2)))
            def _():
                part = held.at[h, src, 2]
                pltpu.make_async_remote_copy(
                    src_ref=part, dst_ref=held.at[h, src, own],
                    send_sem=s2.at[h, 0], recv_sem=r2.at[h, src],
                    device_id=(band, grid), device_id_type=pl.DeviceIdType.MESH,
                ).wait_recv()

    def fourth(h, k):
        q, to_band, to_grid = peer(k)
        return remote(packed.at[h, q], lines.at[h, me], s4.at[h, k], r4.at[h, k], to_band, to_grid)

    def fourth_local(h):
        return pltpu.make_async_copy(packed.at[h, me], lines.at[h, me], loc.at[3 + h])

    def densities(h):
        @pl.loop(0, 2)
        def _(v):
            reals, imags = [], []
            for src in range(n):
                for p in range(2):
                    own_re, own_im = held[h, src, own, 0, p], held[h, src, own, 1, p]
                    vis_re, vis_im = held[h, src, v, 0, p], held[h, src, v, 1, p]
                    reals.append(vis_re * own_re + vis_im * own_im)
                    imags.append(vis_re * own_im - vis_im * own_re)
            pair = jnp.concatenate([jnp.concatenate(reals, axis=0), jnp.concatenate(imags, axis=0)], axis=1)
            value = right(pair, zf_ref)
            for i in range(0, 2 * n, 2):
                both = [
                    jnp.concatenate([value[p * ny:(p + 1) * ny, :nz], value[p * ny:(p + 1) * ny, nz:]], axis=0)
                    for p in (i, i + 1)
                ]
                done = left(yf_ref, jnp.concatenate(both, axis=1))
                for p in range(2):
                    for part in range(2):
                        piece = done[part * ny:(part + 1) * ny, p * nz:(p + 1) * nz]
                        packed[h, :, v, :, part, i + p, :] = piece.reshape(peers, rows, nz)

    for h in range(HALVES):
        hop(h, 3)
        received(h)
        densities(h)
        fourth_local(h).start()
        for k in range(1, peers):
            fourth(h, k).start()
        if h == 0:
            hop(HALVES, 1)
            hop(1, 2)
            hop(HALVES, 2)
    hop(HALVES, 3)

    for h in range(HALVES):
        fourth_local(h).wait()
        for k in range(1, peers):
            fourth(h, k).wait()

    @pl.loop(0, n)
    def _(src):
        for v in range(2):
            for c in range(0, n, 2):
                both = [
                    jnp.concatenate(
                        [lines[:, :, v, src * n + c + p, part].reshape(nx, nz) for part in range(2)], axis=0
                    )
                    for p in range(2)
                ]
                weight = jnp.concatenate([screen[src, c], screen[src, c + 1]], axis=1)
                value = left(xf_ref, jnp.concatenate(both, axis=1))
                value = value * jnp.concatenate([weight, weight], axis=0)
                value = left(xi_ref, value)
                for p in range(2):
                    for part in range(2):
                        piece = value[part * nx:(part + 1) * nx, p * nz:(p + 1) * nz]
                        packed[:, :, v, src * n + c + p, part] = piece.reshape(HALVES, peers, 2 * n, nz)

    def sixth(h, k):
        q, to_band, to_grid = peer(k)
        return remote(packed.at[h, q], back.at[h, me], s6.at[h, k], r6.at[h, k], to_band, to_grid)

    def sixth_local(h):
        return pltpu.make_async_copy(packed.at[h, me], back.at[h, me], loc.at[5 + h])

    def seventh(h, to):
        return remote(result.at[h, to], slab.at[h, z], s7.at[h, to], r7.at[h, z], band, line(to))

    def seventh_local(h, to):
        return pltpu.make_async_copy(result.at[h, to], slab.at[h, to], loc.at[7 + h])

    def out_part(j, h):
        return out_ref.at[0, :, pl.ds(j * n + h * 2, 2)]

    def eighth(h, src):
        return remote(slab.at[h, src], out_part(band, h), s8.at[h, src], r8.at[h, band], PLANE_BAND[src], grid)

    def eighth_local(h, src):
        return pltpu.make_async_copy(slab.at[h, src], out_part(band, h), loc.at[9 + h])

    for h in range(HALVES):
        sixth_local(h).start()
        for k in range(1, peers):
            sixth(h, k).start()

    def deliver(h):
        for src in range(n):
            @pl.when(z == src)
            def _():
                seventh_local(h, src).wait()

            @pl.when(z != src)
            def _():
                pltpu.make_async_remote_copy(
                    src_ref=result.at[h, src], dst_ref=slab.at[h, src],
                    send_sem=s7.at[h, src], recv_sem=r7.at[h, src],
                    device_id=(band, grid), device_id_type=pl.DeviceIdType.MESH,
                ).wait_recv()

            @pl.when(band == PLANE_BAND[src])
            def _():
                eighth_local(h, src).start()

            @pl.when(band != PLANE_BAND[src])
            def _():
                eighth(h, src).start()

    for h in range(HALVES):
        sixth_local(h).wait()
        for k in range(1, peers):
            sixth(h, k).wait_recv()
        for src in range(n):
            for p in range(2):
                i = src * 2 + p
                both = [
                    jnp.concatenate([back[h, :, v, :, part, i, :].reshape(ny, nz) for part in range(2)], axis=0)
                    for v in range(2)
                ]
                value = left(yi_ref, jnp.concatenate(both, axis=1))
                value = jnp.concatenate(
                    [
                        jnp.concatenate([value[:ny, v * nz:(v + 1) * nz], value[ny:, v * nz:(v + 1) * nz]], axis=1)
                        for v in range(2)
                    ],
                    axis=0,
                )
                value = -0.25 * right(value, zi_ref)
                total_re, total_im = 0.0, 0.0
                for v in range(2):
                    pot_re, pot_im = value[v * ny:(v + 1) * ny, :nz], value[v * ny:(v + 1) * ny, nz:]
                    vis_re, vis_im = held[h, src, v, 0, p], held[h, src, v, 1, p]
                    total_re = total_re + (pot_re * vis_re - pot_im * vis_im)
                    total_im = total_im + (pot_re * vis_im + pot_im * vis_re)
                result[h, src, 0, p] = total_re
                result[h, src, 1, p] = total_im

            @pl.when(z == src)
            def _():
                seventh_local(h, src).start()

            @pl.when(z != src)
            def _():
                seventh(h, src).start()
    for h in range(HALVES):
        deliver(h)

    for h in range(HALVES):
        for d in range(1, n):
            first(h, d).wait_send()
        for c in range(2):
            @pl.when(z != c + 1)
            def _():
                direct(h, c).wait_send()
        for k in range(1, peers):
            sixth(h, k).wait_send()
        for src in range(n):
            @pl.when(z != src)
            def _():
                seventh(h, src).wait_send()

            @pl.when(band == PLANE_BAND[src])
            def _():
                eighth_local(h, src).wait()

            @pl.when(band != PLANE_BAND[src])
            def _():
                eighth(h, src).wait_send()

            @pl.when(band != src)
            def _():
                pltpu.make_async_remote_copy(
                    src_ref=slab.at[h, 0], dst_ref=out_part(src, h),
                    send_sem=s8.at[h, src], recv_sem=r8.at[h, src],
                    device_id=(band, grid), device_id_type=pl.DeviceIdType.MESH,
                ).wait_recv()
    for stream in range(HALVES + 1):
        hops_sent(stream)


def fused(bands, coulomb):
    n = GROUPS
    spread = lax.axis_size("grid") // n
    peers = n * spread
    nx, ny, nz = coulomb.shape[0], bands.shape[3], bands.shape[4]
    rows = ny // peers
    q = np.arange(peers)
    row_order = (
        (np.arange(n)[None, :, None] * spread + (q % spread)[:, None, None]) * rows
        + (q // spread)[:, None, None] * n
        + np.arange(n)[None, None, :]
    ).reshape(-1)
    plane_order = (
        np.arange(n)[None, None, :, None] * (nx // n)
        + (q % spread)[None, :, None, None] * (nx // n // spread)
        + (q // spread)[None, :, None, None] * n
        + np.arange(HALVES)[:, None, None, None] * 2
        + np.arange(2)
    ).reshape(-1)
    tabs = [jnp.asarray(t) for t in permuted_tables(nx, 1.0 / (nx * ny * nz), row_order, plane_order)]
    mine = lax.dynamic_slice_in_dim(coulomb, lax.axis_index("band") * n, n, axis=1).transpose(1, 0, 2)
    f32 = jnp.float32
    blocks = (HALVES, peers, 2, rows, 2, 2 * n, nz)
    sem = pltpu.SemaphoreType.DMA
    return pl.pallas_call(
        functools.partial(fused_kernel, spread),
        in_specs=[pl.BlockSpec(memory_space=pl.ANY)] * 2 + [pl.BlockSpec(memory_space=pltpu.VMEM)] * 6,
        out_specs=pl.BlockSpec(memory_space=pl.ANY),
        out_shape=jax.ShapeDtypeStruct(bands.shape, f32),
        scratch_shapes=[
            pltpu.VMEM((HALVES, n, n, 2, 2, ny, nz), f32),
            pltpu.VMEM((n, n, nx, nz), f32),
            pltpu.VMEM(blocks, f32),
            pltpu.VMEM(blocks, f32),
            pltpu.VMEM(blocks, f32),
            pltpu.VMEM((HALVES, n, 2, 2, ny, nz), f32),
            pltpu.VMEM((HALVES, n, 2, 2, ny, nz), f32),
            sem((HALVES, n)), sem((HALVES, n)),
            sem((HALVES, 2)), sem((HALVES, n)),
            sem((HALVES + 1, n)), sem((HALVES + 1, n)),
            sem((HALVES + 1, n)), sem((HALVES + 1, n)),
            sem((HALVES, peers)), sem((HALVES, peers)),
            sem((HALVES, peers)), sem((HALVES, peers)),
            sem((HALVES, n)), sem((HALVES, n)),
            sem((HALVES, n)), sem((HALVES, n)),
            sem((11,)),
        ],
        compiler_params=pltpu.CompilerParams(
            collective_id=0, has_side_effects=True, vmem_limit_bytes=VMEM_LIMIT
        ),
        name="exchange_by_planes",
    )(bands, mine, *tabs)


def fits(bands, coulomb):
    groups, shards = lax.axis_size("band"), lax.axis_size("grid")
    return (
        bands.shape[0] == 1
        and groups == GROUPS
        and shards % GROUPS == 0
        and bands.shape[2] == 2 * HALVES * GROUPS
        and bands.shape[3] == GROUPS * GROUPS * shards
        and coulomb.shape[0] == bands.shape[3] == bands.shape[4]
    )


def body(bands, coulomb):
    if fits(bands, coulomb):
        return fused(bands, coulomb)
    return by_pairs(bands, coulomb)


def solution(mesh):
    in_specs = (P("band", None, "grid", None, None), P(None, "grid", None))
    out_specs = P("band", None, "grid", None, None)
    return jax.shard_map(body, mesh=mesh, in_specs=in_specs, out_specs=out_specs, check_vma=False)
```

```python
import functools

import jax
import jax.numpy as jnp
import ml_dtypes
import numpy as np
from jax import lax
from jax.experimental import pallas as pl
from jax.experimental.pallas import tpu as pltpu
from jax.sharding import PartitionSpec as P

STEPS = 2
VMEM_LIMIT = 48 * 1024 * 1024


def split_table(table):
    high = table.astype(ml_dtypes.bfloat16)
    low = (table - high.astype(np.float64)).astype(ml_dtypes.bfloat16)
    return np.stack([high, low])


def tables(length, scale):
    index = np.arange(length)
    angle = (index[:, None] * index[None, :] % length) * (2.0 * np.pi / length)
    cosine, sine = np.cos(angle), np.sin(angle)
    forward = np.block([[cosine, sine], [-sine, cosine]])
    inverse = np.block([[cosine, -sine], [sine, cosine]])
    return [split_table(t) for t in (forward, inverse, inverse * scale, forward.T, inverse.T)]


def split(values):
    high = values.astype(jnp.bfloat16)
    return high, (values - high.astype(jnp.float32)).astype(jnp.bfloat16)


def dot(a, b):
    return jnp.dot(a, b, preferred_element_type=jnp.float32)


def left(table_ref, values):
    high, low = split(values)
    return dot(table_ref[0], high) + (dot(table_ref[1], high) + dot(table_ref[0], low))


def right(values, table_ref):
    high, low = split(values)
    return dot(high, table_ref[0]) + (dot(high, table_ref[1]) + dot(low, table_ref[0]))


def forward_kernel(own_ref, vis_ref, left_ref, right_ref, out_ref):
    planes, ny, nz = own_ref.shape[2:]
    shards, _, rows = out_ref.shape[:3]
    own_re, own_im, vis_re, vis_im = own_ref[0, 0], own_ref[0, 1], vis_ref[0, 0], vis_ref[0, 1]
    real = vis_re * own_re + vis_im * own_im
    imag = vis_re * own_im - vis_im * own_re
    pair = jnp.concatenate([real.reshape(planes * ny, nz), imag.reshape(planes * ny, nz)], axis=1)
    lines = right(pair, right_ref)
    for i in range(0, planes, 2):
        both = [
            jnp.concatenate([lines[p * ny:(p + 1) * ny, :nz], lines[p * ny:(p + 1) * ny, nz:]], axis=0)
            for p in (i, i + 1)
        ]
        result = left(left_ref, jnp.concatenate(both, axis=1))
        for p in range(2):
            for part in range(2):
                piece = result[part * ny:(part + 1) * ny, p * nz:(p + 1) * nz]
                out_ref[:, part, :, i + p, :] = piece.reshape(shards, rows, nz)


def pencil_kernel(in_ref, coulomb_ref, forward_ref, inverse_ref, out_ref):
    shards, _, rows, planes, nz = in_ref.shape
    nx = shards * planes
    for k in range(0, rows, 2):
        both = []
        for q in (k, k + 1):
            both.append(
                jnp.concatenate([in_ref[:, part, q].reshape(nx, nz) for part in range(2)], axis=0)
            )
        weight = jnp.concatenate([coulomb_ref[:, k, :], coulomb_ref[:, k + 1, :]], axis=1)
        value = left(forward_ref, jnp.concatenate(both, axis=1))
        value = value * jnp.concatenate([weight, weight], axis=0)
        value = left(inverse_ref, value)
        for q in range(2):
            for part in range(2):
                piece = value[part * nx:(part + 1) * nx, q * nz:(q + 1) * nz]
                out_ref[:, part, k + q] = piece.reshape(shards, planes, nz)


def inverse_kernel(has_base, in_ref, vis_ref, left_ref, right_ref, *rest):
    base_ref, out_ref = rest if has_base else (None, rest[0])
    shards, _, rows, planes, nz = in_ref.shape
    ny = shards * rows
    for i in range(0, planes, 2):
        both = []
        for p in (i, i + 1):
            both.append(
                jnp.concatenate([in_ref[:, part, :, p, :].reshape(ny, nz) for part in range(2)], axis=0)
            )
        result = left(left_ref, jnp.concatenate(both, axis=1))
        for p in range(2):
            cut = result[:, p * nz:(p + 1) * nz]
            value = right(jnp.concatenate([cut[:ny], cut[ny:]], axis=1), right_ref)
            pot_re, pot_im = -0.25 * value[:, :nz], -0.25 * value[:, nz:]
            vis_re, vis_im = vis_ref[0, 0, i + p], vis_ref[0, 1, i + p]
            out_re = pot_re * vis_re - pot_im * vis_im
            out_im = pot_re * vis_im + pot_im * vis_re
            if has_base:
                out_re = out_re + base_ref[0, 0, i + p]
                out_im = out_im + base_ref[0, 1, i + p]
            out_ref[0, 0, i + p] = out_re
            out_ref[0, 1, i + p] = out_im


def whole_spec(array):
    return pl.BlockSpec(array.shape, lambda i: (0,) * array.ndim)


def forward(own, vis, shards, tabs):
    _, _, planes, ny, nz = own.shape
    step = min(8, planes)
    slab = pl.BlockSpec((1, 2, step, ny, nz), lambda i: (0, 0, i, 0, 0))
    return pl.pallas_call(
        forward_kernel,
        grid=(planes // step,),
        in_specs=[slab, slab, whole_spec(tabs[0]), whole_spec(tabs[3])],
        out_specs=pl.BlockSpec((shards, 2, ny // shards, step, nz), lambda i: (0, 0, 0, i, 0)),
        out_shape=jax.ShapeDtypeStruct((shards, 2, ny // shards, planes, nz), jnp.float32),
        compiler_params=pltpu.CompilerParams(vmem_limit_bytes=VMEM_LIMIT),
        name="pair_density_dft",
    )(own, vis, tabs[0], tabs[3])


def pencil(block, coulomb, tabs):
    shards, _, rows, planes, nz = block.shape
    step = min(8, rows)
    spec = pl.BlockSpec((shards, 2, step, planes, nz), lambda i: (0, 0, i, 0, 0))
    return pl.pallas_call(
        pencil_kernel,
        grid=(rows // step,),
        in_specs=[
            spec,
            pl.BlockSpec((coulomb.shape[0], step, nz), lambda i: (0, i, 0)),
            whole_spec(tabs[0]),
            whole_spec(tabs[2]),
        ],
        out_specs=spec,
        out_shape=jax.ShapeDtypeStruct(block.shape, jnp.float32),
        compiler_params=pltpu.CompilerParams(vmem_limit_bytes=VMEM_LIMIT),
        name="screen_pencils",
    )(block, coulomb, tabs[0], tabs[2])


def inverse(block, vis, base, tabs):
    shards, _, rows, planes, nz = block.shape
    step = min(8, planes)
    slab = pl.BlockSpec((1, 2, step, shards * rows, nz), lambda i: (0, 0, i, 0, 0))
    extra = [] if base is None else [base]
    return pl.pallas_call(
        functools.partial(inverse_kernel, base is not None),
        grid=(planes // step,),
        in_specs=[
            pl.BlockSpec((shards, 2, rows, step, nz), lambda i: (0, 0, 0, i, 0)),
            slab,
            whole_spec(tabs[1]),
            whole_spec(tabs[4]),
        ] + [slab] * len(extra),
        out_specs=slab,
        out_shape=jax.ShapeDtypeStruct(vis.shape, jnp.float32),
        compiler_params=pltpu.CompilerParams(vmem_limit_bytes=VMEM_LIMIT),
        name="potential_to_exchange",
    )(block, vis, tabs[1], tabs[4], *extra)


def by_pairs(bands, coulomb):
    groups = lax.axis_size("band")
    shards = lax.axis_size("grid")
    span = groups // STEPS
    nx, ny, nz = coulomb.shape[0], bands.shape[3], bands.shape[4]
    tabs = [jnp.asarray(t) for t in tables(nx, 1.0 / (nx * ny * nz))]

    place = lax.axis_index("band") % span
    near = bands
    reach = 1
    while reach < span:
        moves = [(s * span + i, s * span + i + reach) for s in range(STEPS) for i in range(min(reach, span - reach))]
        arrived = lax.ppermute(near, "band", moves)
        near = jnp.where((place >= reach) & (place < 2 * reach), arrived, near)
        reach *= 2
    visitors = [near]
    for _ in range(STEPS - 1):
        visitors.append(lax.ppermute(visitors[-1], "band", [(i, (i + span) % groups) for i in range(groups)]))

    total = None
    sent = [forward(bands, vis, shards, tabs) for vis in visitors]
    sent = [lax.all_to_all(s, "grid", 0, 0, tiled=True) for s in sent]
    sent = [pencil(s, coulomb, tabs) for s in sent]
    sent = [lax.all_to_all(s, "grid", 0, 0, tiled=True) for s in sent]
    for block, vis in zip(sent, visitors):
        total = inverse(block, vis, total, tabs)
    return total


def permuted_tables(length, scale, row_order, plane_order):
    index = np.arange(length)
    angle = (index[:, None] * index[None, :] % length) * (2.0 * np.pi / length)
    cosine, sine = np.cos(angle), np.sin(angle)
    forward = np.block([[cosine, sine], [-sine, cosine]])
    inverse = np.block([[cosine, -sine], [sine, cosine]])
    rows = np.concatenate([row_order, row_order + length])
    planes = np.concatenate([plane_order, plane_order + length])
    return [
        split_table(t)
        for t in (
            forward.T,
            forward[rows],
            forward[:, planes],
            inverse[planes] * scale,
            inverse[:, rows],
            inverse.T,
        )
    ]


GROUPS = 4
HALVES = 2
PLANE_BAND = (0, 1, 3, 2)
PLANE_SLOT = (0, 2, 3, 1)


def fused_kernel(
    spread,
    bands_ref, coulomb_ref, tables_ref,
    out_ref,
    tabs, held, screen, packed, lines, back, result, slab,
    s1, r1, s2, r2, su, ru, sd, rd, s4, r4, s6, r6, s7, r7, s8, r8, loc,
):
    n = GROUPS
    peers = n * spread
    zf_ref, yf_ref, xf_ref, xi_ref, yi_ref, zi_ref = (tabs.at[i] for i in range(6))
    band = lax.axis_index("band")
    grid = lax.axis_index("grid")
    z = grid // spread
    t = grid % spread
    me = band * spread + t
    ny, nz = bands_ref.shape[3], bands_ref.shape[4]
    rows = ny // peers
    nx = peers * 2 * n * HALVES

    def remote(src, dst, send, recv, to_band, to_grid):
        return pltpu.make_async_remote_copy(
            src_ref=src, dst_ref=dst, send_sem=send, recv_sem=recv,
            device_id=(to_band, to_grid), device_id_type=pl.DeviceIdType.MESH,
        )

    def peer(k):
        q = (me + k) % peers
        return q, q // spread, z * spread + q % spread

    def line(k):
        return k * spread + t

    barrier = pltpu.get_barrier_semaphore()
    for k in range(1, peers):
        _, to_band, to_grid = peer(k)
        pl.semaphore_signal(barrier, inc=1, device_id=(to_band, to_grid), device_id_type=pl.DeviceIdType.MESH)
    for k in range(1, n):
        pl.semaphore_signal(
            barrier, inc=1, device_id=(band, line((z + k) % n)), device_id_type=pl.DeviceIdType.MESH
        )
    pl.semaphore_wait(barrier, peers - 1 + n - 1)

    slot = (band % 2) * 2 + band // 2

    def chunk(h, j):
        return bands_ref.at[0, :, pl.ds(j * n + h * 2, 2)]

    def first(h, d):
        to = (band + d) % n
        return remote(chunk(h, to), held.at[h, z, slot], s1.at[h, d], r1.at[h, d], to, grid)

    def first_local(h):
        return pltpu.make_async_copy(chunk(h, band), held.at[h, z, slot], loc.at[h])

    screen_local = pltpu.make_async_copy(coulomb_ref, screen.at[z], loc.at[HALVES])
    tables_local = pltpu.make_async_copy(tables_ref, tabs, loc.at[11])

    def first_start(h):
        for d in (2, 1, 3):
            first(h, d).start()
        first_local(h).start()

    def first_wait(h):
        first_local(h).wait()
        for d in range(1, n):
            first(h, d).wait_recv()

    first_start(0)
    screen_local.start()
    tables_local.start()

    def block(stream, src):
        return held.at[stream, src, pl.ds(0, 2)] if stream < HALVES else screen.at[src]

    def up(stream, d):
        return remote(
            block(stream, z - d), block(stream, z - d), su.at[stream, d], ru.at[stream, d], band, line(z + 1)
        )

    def down(stream, d):
        return remote(
            block(stream, z + d), block(stream, z + d), sd.at[stream, d], rd.at[stream, d], band, line(z - 1)
        )

    def hop(stream, d):
        if d > 0:
            @pl.when(z >= d)
            def _():
                pltpu.make_async_remote_copy(
                    src_ref=block(stream, z - d), dst_ref=block(stream, z - d),
                    send_sem=su.at[stream, d], recv_sem=ru.at[stream, d - 1],
                    device_id=(band, grid), device_id_type=pl.DeviceIdType.MESH,
                ).wait_recv()

            @pl.when(z + d < n)
            def _():
                pltpu.make_async_remote_copy(
                    src_ref=block(stream, z + d), dst_ref=block(stream, z + d),
                    send_sem=sd.at[stream, d], recv_sem=rd.at[stream, d - 1],
                    device_id=(band, grid), device_id_type=pl.DeviceIdType.MESH,
                ).wait_recv()
        if d < n - 1:
            @pl.when((z >= d) & (z + 1 < n))
            def _():
                up(stream, d).start()

            @pl.when((z + d < n) & (z >= 1))
            def _():
                down(stream, d).start()

    def hops_sent(stream):
        for d in range(n - 1):
            @pl.when((z >= d) & (z + 1 < n))
            def _():
                up(stream, d).wait_send()

            @pl.when((z + d < n) & (z >= 1))
            def _():
                down(stream, d).wait_send()

    def direct(h, c):
        to = c + 1
        part = held.at[h, z, 2 + c]
        return remote(part, part, s2.at[h, c], r2.at[h, z], band, line(to))

    def direct_start(h):
        for c in range(2):
            @pl.when(z != c + 1)
            def _():
                direct(h, c).start()

    first_wait(0)
    hop(0, 0)
    first_start(1)
    first_wait(1)
    hop(0, 1)
    direct_start(0)
    hop(1, 0)
    hop(0, 2)
    direct_start(1)
    hop(1, 1)
    screen_local.wait()
    tables_local.wait()

    own = jnp.where(z == 0, 0, jnp.where(z == 1, 2, jnp.where(z == 2, 3, 1)))

    def received(h):
        for src in range(n):
            @pl.when((z != src) & ((z == 1) | (z == 2)))
            def _():
                part = held.at[h, src, 2]
                pltpu.make_async_remote_copy(
                    src_ref=part, dst_ref=held.at[h, src, own],
                    send_sem=s2.at[h, 0], recv_sem=r2.at[h, src],
                    device_id=(band, grid), device_id_type=pl.DeviceIdType.MESH,
                ).wait_recv()

    def fourth(h, v, k):
        q, to_band, to_grid = peer(k)
        return remote(packed.at[h, q, v], lines.at[h, me, v], s4.at[h, v, k], r4.at[h, v, k], to_band, to_grid)

    def fourth_local(h, v):
        return pltpu.make_async_copy(packed.at[h, me, v], lines.at[h, me, v], loc.at[12 + 2 * h + v])

    def densities(h):
        @pl.loop(0, 2)
        def _(v):
            reals, imags = [], []
            for src in range(n):
                for p in range(2):
                    own_re, own_im = held[h, src, own, 0, p], held[h, src, own, 1, p]
                    vis_re, vis_im = held[h, src, v, 0, p], held[h, src, v, 1, p]
                    reals.append(vis_re * own_re + vis_im * own_im)
                    imags.append(vis_re * own_im - vis_im * own_re)
            pair = jnp.concatenate([jnp.concatenate(reals, axis=0), jnp.concatenate(imags, axis=0)], axis=1)
            value = right(pair, zf_ref)
            for i in range(0, 2 * n, 2):
                both = [
                    jnp.concatenate([value[p * ny:(p + 1) * ny, :nz], value[p * ny:(p + 1) * ny, nz:]], axis=0)
                    for p in (i, i + 1)
                ]
                done = left(yf_ref, jnp.concatenate(both, axis=1))
                for p in range(2):
                    for part in range(2):
                        piece = done[part * ny:(part + 1) * ny, p * nz:(p + 1) * nz]
                        packed[h, :, v, :, part, i + p, :] = piece.reshape(peers, rows, nz)

            for k in range(1, peers):
                fourth(h, v, k).start()
            fourth_local(h, v).start()

    hop(0, 3)
    received(0)
    densities(0)
    hop(1, 2)
    hop(HALVES, 0)
    hop(1, 3)
    received(1)
    densities(1)
    for d in range(1, n):
        hop(HALVES, d)

    def sixth(h, v, k):
        q, to_band, to_grid = peer(k)
        return remote(packed.at[h, q, v], back.at[h, me, v], s6.at[h, v, k], r6.at[h, v, k], to_band, to_grid)

    def sixth_local(h, v):
        return pltpu.make_async_copy(packed.at[h, me, v], back.at[h, me, v], loc.at[16 + 2 * h + v])

    def sixth_start(h, v):
        for k in range(1, peers):
            sixth(h, v, k).start()
        sixth_local(h, v).start()

    def sixth_wait(h, v):
        sixth_local(h, v).wait()
        for k in range(1, peers):
            sixth(h, v, k).wait_recv()

    @pl.loop(0, 2)
    def _(v):
        for h in range(HALVES):
            fourth_local(h, v).wait()
            for k in range(1, peers):
                fourth(h, v, k).wait()

        @pl.loop(0, n)
        def _(src):
            for c in range(0, n, 2):
                both = [
                    jnp.concatenate(
                        [lines[:, :, v, src * n + c + p, part].reshape(nx, nz) for part in range(2)], axis=0
                    )
                    for p in range(2)
                ]
                weight = jnp.concatenate([screen[src, c], screen[src, c + 1]], axis=1)
                value = left(xf_ref, jnp.concatenate(both, axis=1))
                value = value * jnp.concatenate([weight, weight], axis=0)
                value = left(xi_ref, value)
                for p in range(2):
                    for part in range(2):
                        piece = value[part * nx:(part + 1) * nx, p * nz:(p + 1) * nz]
                        packed[:, :, v, src * n + c + p, part] = piece.reshape(HALVES, peers, 2 * n, nz)

        sixth_start(0, v)

    def seventh(h, to):
        return remote(result.at[h, to], slab.at[h, z], s7.at[h, to], r7.at[h, z], band, line(to))

    def seventh_local(h, to):
        return pltpu.make_async_copy(result.at[h, to], slab.at[h, to], loc.at[7 + h])

    def out_part(j, h):
        return out_ref.at[0, :, pl.ds(j * n + h * 2, 2)]

    def eighth(h, src):
        return remote(slab.at[h, src], out_part(band, h), s8.at[h, src], r8.at[h, band], PLANE_BAND[src], grid)

    def eighth_local(h, src):
        return pltpu.make_async_copy(slab.at[h, src], out_part(band, h), loc.at[9 + h])

    def deliver(h):
        for src in range(n):
            @pl.when(z == src)
            def _():
                seventh_local(h, src).wait()

            @pl.when(z != src)
            def _():
                pltpu.make_async_remote_copy(
                    src_ref=result.at[h, src], dst_ref=slab.at[h, src],
                    send_sem=s7.at[h, src], recv_sem=r7.at[h, src],
                    device_id=(band, grid), device_id_type=pl.DeviceIdType.MESH,
                ).wait_recv()

            @pl.when(band == PLANE_BAND[src])
            def _():
                eighth_local(h, src).start()

            @pl.when(band != PLANE_BAND[src])
            def _():
                eighth(h, src).start()

    for h in range(HALVES):
        for v in range(2):
            sixth_wait(h, v)
            if h == 0:
                sixth_start(1, v)
        for src in range(n):
            for p in range(2):
                i = src * 2 + p
                both = [
                    jnp.concatenate([back[h, :, v, :, part, i, :].reshape(ny, nz) for part in range(2)], axis=0)
                    for v in range(2)
                ]
                value = left(yi_ref, jnp.concatenate(both, axis=1))
                value = jnp.concatenate(
                    [
                        jnp.concatenate([value[:ny, v * nz:(v + 1) * nz], value[ny:, v * nz:(v + 1) * nz]], axis=1)
                        for v in range(2)
                    ],
                    axis=0,
                )
                value = -0.25 * right(value, zi_ref)
                total_re, total_im = 0.0, 0.0
                for v in range(2):
                    pot_re, pot_im = value[v * ny:(v + 1) * ny, :nz], value[v * ny:(v + 1) * ny, nz:]
                    vis_re, vis_im = held[h, src, v, 0, p], held[h, src, v, 1, p]
                    total_re = total_re + (pot_re * vis_re - pot_im * vis_im)
                    total_im = total_im + (pot_re * vis_im + pot_im * vis_re)
                result[h, src, 0, p] = total_re
                result[h, src, 1, p] = total_im

            @pl.when(z == src)
            def _():
                seventh_local(h, src).start()

            @pl.when(z != src)
            def _():
                seventh(h, src).start()
    for h in range(HALVES):
        deliver(h)

    for h in range(HALVES):
        for d in range(1, n):
            first(h, d).wait_send()
        for c in range(2):
            @pl.when(z != c + 1)
            def _():
                direct(h, c).wait_send()
        for v in range(2):
            for k in range(1, peers):
                sixth(h, v, k).wait_send()
        for src in range(n):
            @pl.when(z != src)
            def _():
                seventh(h, src).wait_send()

            @pl.when(band == PLANE_BAND[src])
            def _():
                eighth_local(h, src).wait()

            @pl.when(band != PLANE_BAND[src])
            def _():
                eighth(h, src).wait_send()

            @pl.when(band != src)
            def _():
                pltpu.make_async_remote_copy(
                    src_ref=slab.at[h, 0], dst_ref=out_part(src, h),
                    send_sem=s8.at[h, src], recv_sem=r8.at[h, src],
                    device_id=(band, grid), device_id_type=pl.DeviceIdType.MESH,
                ).wait_recv()
    for stream in range(HALVES + 1):
        hops_sent(stream)


def fused(bands, coulomb):
    n = GROUPS
    spread = lax.axis_size("grid") // n
    peers = n * spread
    nx, ny, nz = coulomb.shape[0], bands.shape[3], bands.shape[4]
    rows = ny // peers
    q = np.arange(peers)
    row_order = (
        (np.arange(n)[None, :, None] * spread + (q % spread)[:, None, None]) * rows
        + (q // spread)[:, None, None] * n
        + np.arange(n)[None, None, :]
    ).reshape(-1)
    plane_order = (
        np.arange(n)[None, None, :, None] * (nx // n)
        + (q % spread)[None, :, None, None] * (nx // n // spread)
        + (q // spread)[None, :, None, None] * n
        + np.arange(HALVES)[:, None, None, None] * 2
        + np.arange(2)
    ).reshape(-1)
    tabs = jnp.asarray(np.stack(permuted_tables(nx, 1.0 / (nx * ny * nz), row_order, plane_order)))
    mine = lax.dynamic_slice_in_dim(coulomb, lax.axis_index("band") * n, n, axis=1).transpose(1, 0, 2)
    f32 = jnp.float32
    blocks = (HALVES, peers, 2, rows, 2, 2 * n, nz)
    sem = pltpu.SemaphoreType.DMA
    return pl.pallas_call(
        functools.partial(fused_kernel, spread),
        in_specs=[pl.BlockSpec(memory_space=pl.ANY)] * 3,
        out_specs=pl.BlockSpec(memory_space=pl.ANY),
        out_shape=jax.ShapeDtypeStruct(bands.shape, f32),
        scratch_shapes=[
            pltpu.VMEM(tabs.shape, tabs.dtype),
            pltpu.VMEM((HALVES, n, n, 2, 2, ny, nz), f32),
            pltpu.VMEM((n, n, nx, nz), f32),
            pltpu.VMEM(blocks, f32),
            pltpu.VMEM(blocks, f32),
            pltpu.VMEM(blocks, f32),
            pltpu.VMEM((HALVES, n, 2, 2, ny, nz), f32),
            pltpu.VMEM((HALVES, n, 2, 2, ny, nz), f32),
            sem((HALVES, n)), sem((HALVES, n)),
            sem((HALVES, 2)), sem((HALVES, n)),
            sem((HALVES + 1, n)), sem((HALVES + 1, n)),
            sem((HALVES + 1, n)), sem((HALVES + 1, n)),
            sem((HALVES, 2, peers)), sem((HALVES, 2, peers)),
            sem((HALVES, 2, peers)), sem((HALVES, 2, peers)),
            sem((HALVES, n)), sem((HALVES, n)),
            sem((HALVES, n)), sem((HALVES, n)),
            sem((20,)),
        ],
        compiler_params=pltpu.CompilerParams(
            collective_id=0, has_side_effects=True, vmem_limit_bytes=58 * 1024 * 1024
        ),
        name="exchange_by_planes",
    )(bands, mine, tabs)


def fits(bands, coulomb):
    groups, shards = lax.axis_size("band"), lax.axis_size("grid")
    return (
        bands.shape[0] == 1
        and groups == GROUPS
        and shards % GROUPS == 0
        and bands.shape[2] == 2 * HALVES * GROUPS
        and bands.shape[3] == GROUPS * GROUPS * shards
        and coulomb.shape[0] == bands.shape[3] == bands.shape[4]
    )


def body(bands, coulomb):
    if fits(bands, coulomb):
        return fused(bands, coulomb)
    return by_pairs(bands, coulomb)


def solution(mesh):
    in_specs = (P("band", None, "grid", None, None), P(None, "grid", None))
    out_specs = P("band", None, "grid", None, None)
    return jax.shard_map(body, mesh=mesh, in_specs=in_specs, out_specs=out_specs, check_vma=False)
```

```python
import functools

import jax
import jax.numpy as jnp
import ml_dtypes
import numpy as np
from jax import lax
from jax.experimental import pallas as pl
from jax.experimental.pallas import tpu as pltpu
from jax.sharding import PartitionSpec as P

STEPS = 2
VMEM_LIMIT = 48 * 1024 * 1024


def split_table(table):
    high = table.astype(ml_dtypes.bfloat16)
    low = (table - high.astype(np.float64)).astype(ml_dtypes.bfloat16)
    return np.stack([high, low])


def tables(length, scale):
    index = np.arange(length)
    angle = (index[:, None] * index[None, :] % length) * (2.0 * np.pi / length)
    cosine, sine = np.cos(angle), np.sin(angle)
    forward = np.block([[cosine, sine], [-sine, cosine]])
    inverse = np.block([[cosine, -sine], [sine, cosine]])
    return [split_table(t) for t in (forward, inverse, inverse * scale, forward.T, inverse.T)]


def split(values):
    high = values.astype(jnp.bfloat16)
    return high, (values - high.astype(jnp.float32)).astype(jnp.bfloat16)


def dot(a, b):
    return jnp.dot(a, b, preferred_element_type=jnp.float32)


def left(table_ref, values):
    high, low = split(values)
    return dot(table_ref[0], high) + (dot(table_ref[1], high) + dot(table_ref[0], low))


def right(values, table_ref):
    high, low = split(values)
    return dot(high, table_ref[0]) + (dot(high, table_ref[1]) + dot(low, table_ref[0]))


def forward_kernel(own_ref, vis_ref, left_ref, right_ref, out_ref):
    planes, ny, nz = own_ref.shape[2:]
    shards, _, rows = out_ref.shape[:3]
    own_re, own_im, vis_re, vis_im = own_ref[0, 0], own_ref[0, 1], vis_ref[0, 0], vis_ref[0, 1]
    real = vis_re * own_re + vis_im * own_im
    imag = vis_re * own_im - vis_im * own_re
    pair = jnp.concatenate([real.reshape(planes * ny, nz), imag.reshape(planes * ny, nz)], axis=1)
    lines = right(pair, right_ref)
    for i in range(0, planes, 2):
        both = [
            jnp.concatenate([lines[p * ny:(p + 1) * ny, :nz], lines[p * ny:(p + 1) * ny, nz:]], axis=0)
            for p in (i, i + 1)
        ]
        result = left(left_ref, jnp.concatenate(both, axis=1))
        for p in range(2):
            for part in range(2):
                piece = result[part * ny:(part + 1) * ny, p * nz:(p + 1) * nz]
                out_ref[:, part, :, i + p, :] = piece.reshape(shards, rows, nz)


def pencil_kernel(in_ref, coulomb_ref, forward_ref, inverse_ref, out_ref):
    shards, _, rows, planes, nz = in_ref.shape
    nx = shards * planes
    for k in range(0, rows, 2):
        both = []
        for q in (k, k + 1):
            both.append(
                jnp.concatenate([in_ref[:, part, q].reshape(nx, nz) for part in range(2)], axis=0)
            )
        weight = jnp.concatenate([coulomb_ref[:, k, :], coulomb_ref[:, k + 1, :]], axis=1)
        value = left(forward_ref, jnp.concatenate(both, axis=1))
        value = value * jnp.concatenate([weight, weight], axis=0)
        value = left(inverse_ref, value)
        for q in range(2):
            for part in range(2):
                piece = value[part * nx:(part + 1) * nx, q * nz:(q + 1) * nz]
                out_ref[:, part, k + q] = piece.reshape(shards, planes, nz)


def inverse_kernel(has_base, in_ref, vis_ref, left_ref, right_ref, *rest):
    base_ref, out_ref = rest if has_base else (None, rest[0])
    shards, _, rows, planes, nz = in_ref.shape
    ny = shards * rows
    for i in range(0, planes, 2):
        both = []
        for p in (i, i + 1):
            both.append(
                jnp.concatenate([in_ref[:, part, :, p, :].reshape(ny, nz) for part in range(2)], axis=0)
            )
        result = left(left_ref, jnp.concatenate(both, axis=1))
        for p in range(2):
            cut = result[:, p * nz:(p + 1) * nz]
            value = right(jnp.concatenate([cut[:ny], cut[ny:]], axis=1), right_ref)
            pot_re, pot_im = -0.25 * value[:, :nz], -0.25 * value[:, nz:]
            vis_re, vis_im = vis_ref[0, 0, i + p], vis_ref[0, 1, i + p]
            out_re = pot_re * vis_re - pot_im * vis_im
            out_im = pot_re * vis_im + pot_im * vis_re
            if has_base:
                out_re = out_re + base_ref[0, 0, i + p]
                out_im = out_im + base_ref[0, 1, i + p]
            out_ref[0, 0, i + p] = out_re
            out_ref[0, 1, i + p] = out_im


def whole_spec(array):
    return pl.BlockSpec(array.shape, lambda i: (0,) * array.ndim)


def forward(own, vis, shards, tabs):
    _, _, planes, ny, nz = own.shape
    step = min(8, planes)
    slab = pl.BlockSpec((1, 2, step, ny, nz), lambda i: (0, 0, i, 0, 0))
    return pl.pallas_call(
        forward_kernel,
        grid=(planes // step,),
        in_specs=[slab, slab, whole_spec(tabs[0]), whole_spec(tabs[3])],
        out_specs=pl.BlockSpec((shards, 2, ny // shards, step, nz), lambda i: (0, 0, 0, i, 0)),
        out_shape=jax.ShapeDtypeStruct((shards, 2, ny // shards, planes, nz), jnp.float32),
        compiler_params=pltpu.CompilerParams(vmem_limit_bytes=VMEM_LIMIT),
        name="pair_density_dft",
    )(own, vis, tabs[0], tabs[3])


def pencil(block, coulomb, tabs):
    shards, _, rows, planes, nz = block.shape
    step = min(8, rows)
    spec = pl.BlockSpec((shards, 2, step, planes, nz), lambda i: (0, 0, i, 0, 0))
    return pl.pallas_call(
        pencil_kernel,
        grid=(rows // step,),
        in_specs=[
            spec,
            pl.BlockSpec((coulomb.shape[0], step, nz), lambda i: (0, i, 0)),
            whole_spec(tabs[0]),
            whole_spec(tabs[2]),
        ],
        out_specs=spec,
        out_shape=jax.ShapeDtypeStruct(block.shape, jnp.float32),
        compiler_params=pltpu.CompilerParams(vmem_limit_bytes=VMEM_LIMIT),
        name="screen_pencils",
    )(block, coulomb, tabs[0], tabs[2])


def inverse(block, vis, base, tabs):
    shards, _, rows, planes, nz = block.shape
    step = min(8, planes)
    slab = pl.BlockSpec((1, 2, step, shards * rows, nz), lambda i: (0, 0, i, 0, 0))
    extra = [] if base is None else [base]
    return pl.pallas_call(
        functools.partial(inverse_kernel, base is not None),
        grid=(planes // step,),
        in_specs=[
            pl.BlockSpec((shards, 2, rows, step, nz), lambda i: (0, 0, 0, i, 0)),
            slab,
            whole_spec(tabs[1]),
            whole_spec(tabs[4]),
        ] + [slab] * len(extra),
        out_specs=slab,
        out_shape=jax.ShapeDtypeStruct(vis.shape, jnp.float32),
        compiler_params=pltpu.CompilerParams(vmem_limit_bytes=VMEM_LIMIT),
        name="potential_to_exchange",
    )(block, vis, tabs[1], tabs[4], *extra)


def by_pairs(bands, coulomb):
    groups = lax.axis_size("band")
    shards = lax.axis_size("grid")
    span = groups // STEPS
    nx, ny, nz = coulomb.shape[0], bands.shape[3], bands.shape[4]
    tabs = [jnp.asarray(t) for t in tables(nx, 1.0 / (nx * ny * nz))]

    place = lax.axis_index("band") % span
    near = bands
    reach = 1
    while reach < span:
        moves = [(s * span + i, s * span + i + reach) for s in range(STEPS) for i in range(min(reach, span - reach))]
        arrived = lax.ppermute(near, "band", moves)
        near = jnp.where((place >= reach) & (place < 2 * reach), arrived, near)
        reach *= 2
    visitors = [near]
    for _ in range(STEPS - 1):
        visitors.append(lax.ppermute(visitors[-1], "band", [(i, (i + span) % groups) for i in range(groups)]))

    total = None
    sent = [forward(bands, vis, shards, tabs) for vis in visitors]
    sent = [lax.all_to_all(s, "grid", 0, 0, tiled=True) for s in sent]
    sent = [pencil(s, coulomb, tabs) for s in sent]
    sent = [lax.all_to_all(s, "grid", 0, 0, tiled=True) for s in sent]
    for block, vis in zip(sent, visitors):
        total = inverse(block, vis, total, tabs)
    return total


def permuted_tables(length, scale, row_order, plane_order):
    index = np.arange(length)
    angle = (index[:, None] * index[None, :] % length) * (2.0 * np.pi / length)
    cosine, sine = np.cos(angle), np.sin(angle)
    forward = np.block([[cosine, sine], [-sine, cosine]])
    inverse = np.block([[cosine, -sine], [sine, cosine]])
    rows = np.concatenate([row_order, row_order + length])
    planes = np.concatenate([plane_order, plane_order + length])
    return [
        split_table(t)
        for t in (
            forward.T,
            forward[rows],
            forward[:, planes],
            inverse[planes] * scale,
            inverse[:, rows],
            inverse.T,
        )
    ]


GROUPS = 4
HALVES = 2
PLANE_BAND = (0, 1, 3, 2)
PLANE_SLOT = (0, 2, 3, 1)


def fused_kernel(
    spread,
    bands_ref, coulomb_ref, tables_ref,
    out_ref,
    tabs, held, screen, packed, lines, back, result, slab,
    s1, r1, s2, r2, su, ru, sd, rd, s4, r4, s6, r6, s7, r7, s8, r8, loc,
):
    n = GROUPS
    peers = n * spread
    zf_ref, yf_ref, xf_ref, xi_ref, yi_ref, zi_ref = (tabs.at[i] for i in range(6))
    band = lax.axis_index("band")
    grid = lax.axis_index("grid")
    z = grid // spread
    t = grid % spread
    me = band * spread + t
    ny, nz = bands_ref.shape[3], bands_ref.shape[4]
    rows = ny // peers
    nx = peers * 2 * n * HALVES

    def remote(src, dst, send, recv, to_band, to_grid):
        return pltpu.make_async_remote_copy(
            src_ref=src, dst_ref=dst, send_sem=send, recv_sem=recv,
            device_id=(to_band, to_grid), device_id_type=pl.DeviceIdType.MESH,
        )

    def peer(k):
        q = (me + k) % peers
        return q, q // spread, z * spread + q % spread

    def line(k):
        return k * spread + t

    barrier = pltpu.get_barrier_semaphore()
    for k in range(1, peers):
        _, to_band, to_grid = peer(k)
        pl.semaphore_signal(barrier, inc=1, device_id=(to_band, to_grid), device_id_type=pl.DeviceIdType.MESH)
    for k in range(1, n):
        pl.semaphore_signal(
            barrier, inc=1, device_id=(band, line((z + k) % n)), device_id_type=pl.DeviceIdType.MESH
        )
    pl.semaphore_wait(barrier, peers - 1 + n - 1)

    slot = (band % 2) * 2 + band // 2

    def chunk(h, j):
        return bands_ref.at[0, :, pl.ds(j * n + h * 2, 2)]

    def first(h, d):
        to = (band + d) % n
        return remote(chunk(h, to), held.at[h, z, slot], s1.at[h, d], r1.at[h, d], to, grid)

    def first_local(h):
        return pltpu.make_async_copy(chunk(h, band), held.at[h, z, slot], loc.at[h])

    screen_local = pltpu.make_async_copy(coulomb_ref, screen.at[z], loc.at[HALVES])
    tables_local = pltpu.make_async_copy(tables_ref, tabs, loc.at[11])

    def first_start(h):
        for d in (2, 1, 3):
            first(h, d).start()
        first_local(h).start()

    def first_wait(h):
        first_local(h).wait()
        for d in range(1, n):
            first(h, d).wait_recv()

    first_start(0)
    screen_local.start()
    tables_local.start()

    def block(stream, src):
        return held.at[stream, src, pl.ds(0, 2)] if stream < HALVES else screen.at[src]

    def up(stream, d):
        return remote(
            block(stream, z - d), block(stream, z - d), su.at[stream, d], ru.at[stream, d], band, line(z + 1)
        )

    def down(stream, d):
        return remote(
            block(stream, z + d), block(stream, z + d), sd.at[stream, d], rd.at[stream, d], band, line(z - 1)
        )

    def hop(stream, d):
        if d > 0:
            @pl.when(z >= d)
            def _():
                pltpu.make_async_remote_copy(
                    src_ref=block(stream, z - d), dst_ref=block(stream, z - d),
                    send_sem=su.at[stream, d], recv_sem=ru.at[stream, d - 1],
                    device_id=(band, grid), device_id_type=pl.DeviceIdType.MESH,
                ).wait_recv()

            @pl.when(z + d < n)
            def _():
                pltpu.make_async_remote_copy(
                    src_ref=block(stream, z + d), dst_ref=block(stream, z + d),
                    send_sem=sd.at[stream, d], recv_sem=rd.at[stream, d - 1],
                    device_id=(band, grid), device_id_type=pl.DeviceIdType.MESH,
                ).wait_recv()
        if d < n - 1:
            @pl.when((z >= d) & (z + 1 < n))
            def _():
                up(stream, d).start()

            @pl.when((z + d < n) & (z >= 1))
            def _():
                down(stream, d).start()

    def hops_sent(stream, distances):
        for d in distances:
            @pl.when((z >= d) & (z + 1 < n))
            def _():
                up(stream, d).wait_send()

            @pl.when((z + d < n) & (z >= 1))
            def _():
                down(stream, d).wait_send()

    def direct(h, c):
        to = c + 1
        part = held.at[h, z, 2 + c]
        return remote(part, part, s2.at[h, c], r2.at[h, z], band, line(to))

    def direct_start(h):
        for c in range(2):
            @pl.when(z != c + 1)
            def _():
                direct(h, c).start()

    def direct_sent(h):
        for c in range(2):
            @pl.when(z != c + 1)
            def _():
                direct(h, c).wait_send()

    first_wait(0)
    hop(0, 0)
    first_start(1)
    hop(0, 1)
    hop(0, 2)
    direct_start(0)
    first_wait(1)
    hops_sent(0, (0, 1, 2))
    direct_sent(0)
    hop(1, 0)
    screen_local.wait()
    tables_local.wait()

    own = jnp.where(z == 0, 0, jnp.where(z == 1, 2, jnp.where(z == 2, 3, 1)))

    def received(h):
        for src in range(n):
            @pl.when((z != src) & ((z == 1) | (z == 2)))
            def _():
                part = held.at[h, src, 2]
                pltpu.make_async_remote_copy(
                    src_ref=part, dst_ref=held.at[h, src, own],
                    send_sem=s2.at[h, 0], recv_sem=r2.at[h, src],
                    device_id=(band, grid), device_id_type=pl.DeviceIdType.MESH,
                ).wait_recv()

    def fourth(h, v, k):
        q, to_band, to_grid = peer(k)
        return remote(packed.at[h, q, v], lines.at[h, me, v], s4.at[h, v, k], r4.at[h, v, k], to_band, to_grid)

    def fourth_local(h, v):
        return pltpu.make_async_copy(packed.at[h, me, v], lines.at[h, me, v], loc.at[12 + 2 * h + v])

    def densities(h):
        @pl.loop(0, 2)
        def _(v):
            reals, imags = [], []
            for src in range(n):
                for p in range(2):
                    own_re, own_im = held[h, src, own, 0, p], held[h, src, own, 1, p]
                    vis_re, vis_im = held[h, src, v, 0, p], held[h, src, v, 1, p]
                    reals.append(vis_re * own_re + vis_im * own_im)
                    imags.append(vis_re * own_im - vis_im * own_re)
            pair = jnp.concatenate([jnp.concatenate(reals, axis=0), jnp.concatenate(imags, axis=0)], axis=1)
            value = right(pair, zf_ref)
            for i in range(0, 2 * n, 2):
                both = [
                    jnp.concatenate([value[p * ny:(p + 1) * ny, :nz], value[p * ny:(p + 1) * ny, nz:]], axis=0)
                    for p in (i, i + 1)
                ]
                done = left(yf_ref, jnp.concatenate(both, axis=1))
                for p in range(2):
                    for part in range(2):
                        piece = done[part * ny:(part + 1) * ny, p * nz:(p + 1) * nz]
                        packed[h, :, v, :, part, i + p, :] = piece.reshape(peers, rows, nz)

            for k in range(1, peers):
                fourth(h, v, k).start()
            fourth_local(h, v).start()

    hop(0, 3)
    received(0)
    densities(0)
    hop(1, 1)
    hop(1, 2)
    direct_start(1)
    hops_sent(1, (0, 1, 2))
    direct_sent(1)
    hop(HALVES, 0)
    hop(1, 3)
    received(1)
    densities(1)
    for d in range(1, n):
        hop(HALVES, d)

    def sixth(h, v, k):
        q, to_band, to_grid = peer(k)
        return remote(packed.at[h, q, v], back.at[h, me, v], s6.at[h, v, k], r6.at[h, v, k], to_band, to_grid)

    def sixth_local(h, v):
        return pltpu.make_async_copy(packed.at[h, me, v], back.at[h, me, v], loc.at[16 + 2 * h + v])

    def sixth_start(h, v):
        for k in range(1, peers):
            sixth(h, v, k).start()
        sixth_local(h, v).start()

    def sixth_wait(h, v):
        sixth_local(h, v).wait()
        for k in range(1, peers):
            sixth(h, v, k).wait_recv()

    @pl.loop(0, 2)
    def _(v):
        for h in range(HALVES):
            fourth_local(h, v).wait()
            for k in range(1, peers):
                fourth(h, v, k).wait()

        @pl.loop(0, n)
        def _(src):
            for c in range(0, n, 2):
                both = [
                    jnp.concatenate(
                        [lines[:, :, v, src * n + c + p, part].reshape(nx, nz) for part in range(2)], axis=0
                    )
                    for p in range(2)
                ]
                weight = jnp.concatenate([screen[src, c], screen[src, c + 1]], axis=1)
                value = left(xf_ref, jnp.concatenate(both, axis=1))
                value = value * jnp.concatenate([weight, weight], axis=0)
                value = left(xi_ref, value)
                for p in range(2):
                    for part in range(2):
                        piece = value[part * nx:(part + 1) * nx, p * nz:(p + 1) * nz]
                        packed[:, :, v, src * n + c + p, part] = piece.reshape(HALVES, peers, 2 * n, nz)

        sixth_start(0, v)

    def seventh(h, to):
        return remote(result.at[h, to], slab.at[h, z], s7.at[h, to], r7.at[h, z], band, line(to))

    def seventh_local(h, to):
        return pltpu.make_async_copy(result.at[h, to], slab.at[h, to], loc.at[7 + h])

    def out_part(j, h):
        return out_ref.at[0, :, pl.ds(j * n + h * 2, 2)]

    def eighth(h, src):
        return remote(slab.at[h, src], out_part(band, h), s8.at[h, src], r8.at[h, band], PLANE_BAND[src], grid)

    def eighth_local(h, src):
        return pltpu.make_async_copy(slab.at[h, src], out_part(band, h), loc.at[9 + h])

    def deliver(h):
        for src in range(n):
            @pl.when(z == src)
            def _():
                seventh_local(h, src).wait()

            @pl.when(z != src)
            def _():
                pltpu.make_async_remote_copy(
                    src_ref=result.at[h, src], dst_ref=slab.at[h, src],
                    send_sem=s7.at[h, src], recv_sem=r7.at[h, src],
                    device_id=(band, grid), device_id_type=pl.DeviceIdType.MESH,
                ).wait_recv()

            @pl.when(band == PLANE_BAND[src])
            def _():
                eighth_local(h, src).start()

            @pl.when(band != PLANE_BAND[src])
            def _():
                eighth(h, src).start()

    for h in range(HALVES):
        for v in range(2):
            sixth_wait(h, v)
        if h == 0:
            for v in range(2):
                sixth_start(1, v)
        for src in range(n):
            for p in range(2):
                i = src * 2 + p
                both = [
                    jnp.concatenate([back[h, :, v, :, part, i, :].reshape(ny, nz) for part in range(2)], axis=0)
                    for v in range(2)
                ]
                value = left(yi_ref, jnp.concatenate(both, axis=1))
                value = jnp.concatenate(
                    [
                        jnp.concatenate([value[:ny, v * nz:(v + 1) * nz], value[ny:, v * nz:(v + 1) * nz]], axis=1)
                        for v in range(2)
                    ],
                    axis=0,
                )
                value = -0.25 * right(value, zi_ref)
                total_re, total_im = 0.0, 0.0
                for v in range(2):
                    pot_re, pot_im = value[v * ny:(v + 1) * ny, :nz], value[v * ny:(v + 1) * ny, nz:]
                    vis_re, vis_im = held[h, src, v, 0, p], held[h, src, v, 1, p]
                    total_re = total_re + (pot_re * vis_re - pot_im * vis_im)
                    total_im = total_im + (pot_re * vis_im + pot_im * vis_re)
                result[h, src, 0, p] = total_re
                result[h, src, 1, p] = total_im

            @pl.when(z == src)
            def _():
                seventh_local(h, src).start()

            @pl.when(z != src)
            def _():
                seventh(h, src).start()
    for h in range(HALVES):
        deliver(h)

    for h in range(HALVES):
        for d in range(1, n):
            first(h, d).wait_send()
        for v in range(2):
            for k in range(1, peers):
                sixth(h, v, k).wait_send()
        for src in range(n):
            @pl.when(z != src)
            def _():
                seventh(h, src).wait_send()

            @pl.when(band == PLANE_BAND[src])
            def _():
                eighth_local(h, src).wait()

            @pl.when(band != PLANE_BAND[src])
            def _():
                eighth(h, src).wait_send()

            @pl.when(band != src)
            def _():
                pltpu.make_async_remote_copy(
                    src_ref=slab.at[h, 0], dst_ref=out_part(src, h),
                    send_sem=s8.at[h, src], recv_sem=r8.at[h, src],
                    device_id=(band, grid), device_id_type=pl.DeviceIdType.MESH,
                ).wait_recv()
    hops_sent(HALVES, (0, 1, 2))


def fused(bands, coulomb):
    n = GROUPS
    spread = lax.axis_size("grid") // n
    peers = n * spread
    nx, ny, nz = coulomb.shape[0], bands.shape[3], bands.shape[4]
    rows = ny // peers
    q = np.arange(peers)
    row_order = (
        (np.arange(n)[None, :, None] * spread + (q % spread)[:, None, None]) * rows
        + (q // spread)[:, None, None] * n
        + np.arange(n)[None, None, :]
    ).reshape(-1)
    plane_order = (
        np.arange(n)[None, None, :, None] * (nx // n)
        + (q % spread)[None, :, None, None] * (nx // n // spread)
        + (q // spread)[None, :, None, None] * n
        + np.arange(HALVES)[:, None, None, None] * 2
        + np.arange(2)
    ).reshape(-1)
    tabs = jnp.asarray(np.stack(permuted_tables(nx, 1.0 / (nx * ny * nz), row_order, plane_order)))
    mine = lax.dynamic_slice_in_dim(coulomb, lax.axis_index("band") * n, n, axis=1).transpose(1, 0, 2)
    f32 = jnp.float32
    blocks = (HALVES, peers, 2, rows, 2, 2 * n, nz)
    sem = pltpu.SemaphoreType.DMA
    return pl.pallas_call(
        functools.partial(fused_kernel, spread),
        in_specs=[pl.BlockSpec(memory_space=pl.ANY)] * 3,
        out_specs=pl.BlockSpec(memory_space=pl.ANY),
        out_shape=jax.ShapeDtypeStruct(bands.shape, f32),
        scratch_shapes=[
            pltpu.VMEM(tabs.shape, tabs.dtype),
            pltpu.VMEM((HALVES, n, n, 2, 2, ny, nz), f32),
            pltpu.VMEM((n, n, nx, nz), f32),
            pltpu.VMEM(blocks, f32),
            pltpu.VMEM(blocks, f32),
            pltpu.VMEM(blocks, f32),
            pltpu.VMEM((HALVES, n, 2, 2, ny, nz), f32),
            pltpu.VMEM((HALVES, n, 2, 2, ny, nz), f32),
            sem((HALVES, n)), sem((HALVES, n)),
            sem((HALVES, 2)), sem((HALVES, n)),
            sem((HALVES + 1, n)), sem((HALVES + 1, n)),
            sem((HALVES + 1, n)), sem((HALVES + 1, n)),
            sem((HALVES, 2, peers)), sem((HALVES, 2, peers)),
            sem((HALVES, 2, peers)), sem((HALVES, 2, peers)),
            sem((HALVES, n)), sem((HALVES, n)),
            sem((HALVES, n)), sem((HALVES, n)),
            sem((20,)),
        ],
        compiler_params=pltpu.CompilerParams(
            collective_id=0, has_side_effects=True, vmem_limit_bytes=VMEM_LIMIT
        ),
        name="exchange_by_planes",
    )(bands, mine, tabs)


def fits(bands, coulomb):
    groups, shards = lax.axis_size("band"), lax.axis_size("grid")
    return (
        bands.shape[0] == 1
        and groups == GROUPS
        and shards % GROUPS == 0
        and bands.shape[2] == 2 * HALVES * GROUPS
        and bands.shape[3] == GROUPS * GROUPS * shards
        and coulomb.shape[0] == bands.shape[3] == bands.shape[4]
    )


def body(bands, coulomb):
    if fits(bands, coulomb):
        return fused(bands, coulomb)
    return by_pairs(bands, coulomb)


def solution(mesh):
    in_specs = (P("band", None, "grid", None, None), P(None, "grid", None))
    out_specs = P("band", None, "grid", None, None)
    return jax.shard_map(body, mesh=mesh, in_specs=in_specs, out_specs=out_specs, check_vma=False)
```

```python
import functools

import jax
import jax.numpy as jnp
import ml_dtypes
import numpy as np
from jax import lax
from jax.experimental import pallas as pl
from jax.experimental.pallas import tpu as pltpu
from jax.sharding import PartitionSpec as P

STEPS = 2
VMEM_LIMIT = 48 * 1024 * 1024


def split_table(table):
    high = table.astype(ml_dtypes.bfloat16)
    low = (table - high.astype(np.float64)).astype(ml_dtypes.bfloat16)
    return np.stack([high, low])


def tables(length, scale):
    index = np.arange(length)
    angle = (index[:, None] * index[None, :] % length) * (2.0 * np.pi / length)
    cosine, sine = np.cos(angle), np.sin(angle)
    forward = np.block([[cosine, sine], [-sine, cosine]])
    inverse = np.block([[cosine, -sine], [sine, cosine]])
    return [split_table(t) for t in (forward, inverse, inverse * scale, forward.T, inverse.T)]


def split(values):
    high = values.astype(jnp.bfloat16)
    return high, (values - high.astype(jnp.float32)).astype(jnp.bfloat16)


def dot(a, b):
    return jnp.dot(a, b, preferred_element_type=jnp.float32)


def left(table_ref, values):
    high, low = split(values)
    return dot(table_ref[0], high) + (dot(table_ref[1], high) + dot(table_ref[0], low))


def right(values, table_ref):
    high, low = split(values)
    return dot(high, table_ref[0]) + (dot(high, table_ref[1]) + dot(low, table_ref[0]))


def forward_kernel(own_ref, vis_ref, left_ref, right_ref, out_ref):
    planes, ny, nz = own_ref.shape[2:]
    shards, _, rows = out_ref.shape[:3]
    own_re, own_im, vis_re, vis_im = own_ref[0, 0], own_ref[0, 1], vis_ref[0, 0], vis_ref[0, 1]
    real = vis_re * own_re + vis_im * own_im
    imag = vis_re * own_im - vis_im * own_re
    pair = jnp.concatenate([real.reshape(planes * ny, nz), imag.reshape(planes * ny, nz)], axis=1)
    lines = right(pair, right_ref)
    for i in range(0, planes, 2):
        both = [
            jnp.concatenate([lines[p * ny:(p + 1) * ny, :nz], lines[p * ny:(p + 1) * ny, nz:]], axis=0)
            for p in (i, i + 1)
        ]
        result = left(left_ref, jnp.concatenate(both, axis=1))
        for p in range(2):
            for part in range(2):
                piece = result[part * ny:(part + 1) * ny, p * nz:(p + 1) * nz]
                out_ref[:, part, :, i + p, :] = piece.reshape(shards, rows, nz)


def pencil_kernel(in_ref, coulomb_ref, forward_ref, inverse_ref, out_ref):
    shards, _, rows, planes, nz = in_ref.shape
    nx = shards * planes
    for k in range(0, rows, 2):
        both = []
        for q in (k, k + 1):
            both.append(
                jnp.concatenate([in_ref[:, part, q].reshape(nx, nz) for part in range(2)], axis=0)
            )
        weight = jnp.concatenate([coulomb_ref[:, k, :], coulomb_ref[:, k + 1, :]], axis=1)
        value = left(forward_ref, jnp.concatenate(both, axis=1))
        value = value * jnp.concatenate([weight, weight], axis=0)
        value = left(inverse_ref, value)
        for q in range(2):
            for part in range(2):
                piece = value[part * nx:(part + 1) * nx, q * nz:(q + 1) * nz]
                out_ref[:, part, k + q] = piece.reshape(shards, planes, nz)


def inverse_kernel(has_base, in_ref, vis_ref, left_ref, right_ref, *rest):
    base_ref, out_ref = rest if has_base else (None, rest[0])
    shards, _, rows, planes, nz = in_ref.shape
    ny = shards * rows
    for i in range(0, planes, 2):
        both = []
        for p in (i, i + 1):
            both.append(
                jnp.concatenate([in_ref[:, part, :, p, :].reshape(ny, nz) for part in range(2)], axis=0)
            )
        result = left(left_ref, jnp.concatenate(both, axis=1))
        for p in range(2):
            cut = result[:, p * nz:(p + 1) * nz]
            value = right(jnp.concatenate([cut[:ny], cut[ny:]], axis=1), right_ref)
            pot_re, pot_im = -0.25 * value[:, :nz], -0.25 * value[:, nz:]
            vis_re, vis_im = vis_ref[0, 0, i + p], vis_ref[0, 1, i + p]
            out_re = pot_re * vis_re - pot_im * vis_im
            out_im = pot_re * vis_im + pot_im * vis_re
            if has_base:
                out_re = out_re + base_ref[0, 0, i + p]
                out_im = out_im + base_ref[0, 1, i + p]
            out_ref[0, 0, i + p] = out_re
            out_ref[0, 1, i + p] = out_im


def whole_spec(array):
    return pl.BlockSpec(array.shape, lambda i: (0,) * array.ndim)


def forward(own, vis, shards, tabs):
    _, _, planes, ny, nz = own.shape
    step = min(8, planes)
    slab = pl.BlockSpec((1, 2, step, ny, nz), lambda i: (0, 0, i, 0, 0))
    return pl.pallas_call(
        forward_kernel,
        grid=(planes // step,),
        in_specs=[slab, slab, whole_spec(tabs[0]), whole_spec(tabs[3])],
        out_specs=pl.BlockSpec((shards, 2, ny // shards, step, nz), lambda i: (0, 0, 0, i, 0)),
        out_shape=jax.ShapeDtypeStruct((shards, 2, ny // shards, planes, nz), jnp.float32),
        compiler_params=pltpu.CompilerParams(vmem_limit_bytes=VMEM_LIMIT),
        name="pair_density_dft",
    )(own, vis, tabs[0], tabs[3])


def pencil(block, coulomb, tabs):
    shards, _, rows, planes, nz = block.shape
    step = min(8, rows)
    spec = pl.BlockSpec((shards, 2, step, planes, nz), lambda i: (0, 0, i, 0, 0))
    return pl.pallas_call(
        pencil_kernel,
        grid=(rows // step,),
        in_specs=[
            spec,
            pl.BlockSpec((coulomb.shape[0], step, nz), lambda i: (0, i, 0)),
            whole_spec(tabs[0]),
            whole_spec(tabs[2]),
        ],
        out_specs=spec,
        out_shape=jax.ShapeDtypeStruct(block.shape, jnp.float32),
        compiler_params=pltpu.CompilerParams(vmem_limit_bytes=VMEM_LIMIT),
        name="screen_pencils",
    )(block, coulomb, tabs[0], tabs[2])


def inverse(block, vis, base, tabs):
    shards, _, rows, planes, nz = block.shape
    step = min(8, planes)
    slab = pl.BlockSpec((1, 2, step, shards * rows, nz), lambda i: (0, 0, i, 0, 0))
    extra = [] if base is None else [base]
    return pl.pallas_call(
        functools.partial(inverse_kernel, base is not None),
        grid=(planes // step,),
        in_specs=[
            pl.BlockSpec((shards, 2, rows, step, nz), lambda i: (0, 0, 0, i, 0)),
            slab,
            whole_spec(tabs[1]),
            whole_spec(tabs[4]),
        ] + [slab] * len(extra),
        out_specs=slab,
        out_shape=jax.ShapeDtypeStruct(vis.shape, jnp.float32),
        compiler_params=pltpu.CompilerParams(vmem_limit_bytes=VMEM_LIMIT),
        name="potential_to_exchange",
    )(block, vis, tabs[1], tabs[4], *extra)


def by_pairs(bands, coulomb):
    groups = lax.axis_size("band")
    shards = lax.axis_size("grid")
    span = groups // STEPS
    nx, ny, nz = coulomb.shape[0], bands.shape[3], bands.shape[4]
    tabs = [jnp.asarray(t) for t in tables(nx, 1.0 / (nx * ny * nz))]

    place = lax.axis_index("band") % span
    near = bands
    reach = 1
    while reach < span:
        moves = [(s * span + i, s * span + i + reach) for s in range(STEPS) for i in range(min(reach, span - reach))]
        arrived = lax.ppermute(near, "band", moves)
        near = jnp.where((place >= reach) & (place < 2 * reach), arrived, near)
        reach *= 2
    visitors = [near]
    for _ in range(STEPS - 1):
        visitors.append(lax.ppermute(visitors[-1], "band", [(i, (i + span) % groups) for i in range(groups)]))

    total = None
    sent = [forward(bands, vis, shards, tabs) for vis in visitors]
    sent = [lax.all_to_all(s, "grid", 0, 0, tiled=True) for s in sent]
    sent = [pencil(s, coulomb, tabs) for s in sent]
    sent = [lax.all_to_all(s, "grid", 0, 0, tiled=True) for s in sent]
    for block, vis in zip(sent, visitors):
        total = inverse(block, vis, total, tabs)
    return total


def permuted_tables(length, scale, row_order, plane_order):
    index = np.arange(length)
    angle = (index[:, None] * index[None, :] % length) * (2.0 * np.pi / length)
    cosine, sine = np.cos(angle), np.sin(angle)
    forward = np.block([[cosine, sine], [-sine, cosine]])
    inverse = np.block([[cosine, -sine], [sine, cosine]])
    rows = np.concatenate([row_order, row_order + length])
    planes = np.concatenate([plane_order, plane_order + length])
    return [
        split_table(t)
        for t in (
            forward.T,
            forward[rows],
            forward[:, planes],
            inverse[planes] * scale,
            inverse[:, rows],
            inverse.T,
        )
    ]


GROUPS = 4
ROUNDS = 4
PLANES = GROUPS // ROUNDS
PLANE_BAND = (0, 1, 3, 2)
PLANE_SLOT = (0, 2, 3, 1)


def fused_kernel(
    spread,
    bands_ref, coulomb_ref, tables_ref,
    out_ref,
    tabs, held, screen, packed, lines, back, result, slab,
    s1, r1, s2, r2, su, ru, sd, rd, s4, r4, s6, r6, s7, r7, s8, r8, loc,
):
    n = GROUPS
    peers = n * spread
    zf_ref, yf_ref, xf_ref, xi_ref, yi_ref, zi_ref = (tabs.at[i] for i in range(6))
    band = lax.axis_index("band")
    grid = lax.axis_index("grid")
    z = grid // spread
    t = grid % spread
    me = band * spread + t
    ny, nz = bands_ref.shape[3], bands_ref.shape[4]
    rows = ny // peers
    nx = peers * n * PLANES * ROUNDS

    def remote(src, dst, send, recv, to_band, to_grid):
        return pltpu.make_async_remote_copy(
            src_ref=src, dst_ref=dst, send_sem=send, recv_sem=recv,
            device_id=(to_band, to_grid), device_id_type=pl.DeviceIdType.MESH,
        )

    def peer(k):
        q = (me + k) % peers
        return q, q // spread, z * spread + q % spread

    def line(k):
        return k * spread + t

    barrier = pltpu.get_barrier_semaphore()
    for k in range(1, peers):
        _, to_band, to_grid = peer(k)
        pl.semaphore_signal(barrier, inc=1, device_id=(to_band, to_grid), device_id_type=pl.DeviceIdType.MESH)
    for k in range(1, n):
        pl.semaphore_signal(
            barrier, inc=1, device_id=(band, line((z + k) % n)), device_id_type=pl.DeviceIdType.MESH
        )
    pl.semaphore_wait(barrier, peers - 1 + n - 1)

    slot = (band % 2) * 2 + band // 2

    def chunk(h, j):
        return bands_ref.at[0, :, pl.ds(j * n + h * PLANES, PLANES)]

    def first(h, d):
        to = (band + d) % n
        return remote(chunk(h, to), held.at[h, z, slot], s1.at[h, d], r1.at[h, d], to, grid)

    def first_local(h):
        return pltpu.make_async_copy(chunk(h, band), held.at[h, z, slot], loc.at[0, h])

    screen_local = pltpu.make_async_copy(coulomb_ref, screen.at[z], loc.at[1, 0])
    tables_local = pltpu.make_async_copy(tables_ref, tabs, loc.at[1, 1])

    def first_start(h):
        for d in (2, 1, 3):
            first(h, d).start()
        first_local(h).start()

    def first_wait(h):
        first_local(h).wait()
        for d in range(1, n):
            first(h, d).wait_recv()

    first_start(0)
    screen_local.start()
    tables_local.start()

    def block(stream, src):
        return held.at[stream, src, pl.ds(0, 2)] if stream < ROUNDS else screen.at[src]

    def up(stream, d):
        return remote(
            block(stream, z - d), block(stream, z - d), su.at[stream, d], ru.at[stream, d], band, line(z + 1)
        )

    def down(stream, d):
        return remote(
            block(stream, z + d), block(stream, z + d), sd.at[stream, d], rd.at[stream, d], band, line(z - 1)
        )

    def hop(stream, d):
        if d > 0:
            @pl.when(z >= d)
            def _():
                pltpu.make_async_remote_copy(
                    src_ref=block(stream, z - d), dst_ref=block(stream, z - d),
                    send_sem=su.at[stream, d], recv_sem=ru.at[stream, d - 1],
                    device_id=(band, grid), device_id_type=pl.DeviceIdType.MESH,
                ).wait_recv()

            @pl.when(z + d < n)
            def _():
                pltpu.make_async_remote_copy(
                    src_ref=block(stream, z + d), dst_ref=block(stream, z + d),
                    send_sem=sd.at[stream, d], recv_sem=rd.at[stream, d - 1],
                    device_id=(band, grid), device_id_type=pl.DeviceIdType.MESH,
                ).wait_recv()
        if d < n - 1:
            @pl.when((z >= d) & (z + 1 < n))
            def _():
                up(stream, d).start()

            @pl.when((z + d < n) & (z >= 1))
            def _():
                down(stream, d).start()

    def hops_sent(stream, distances):
        for d in distances:
            @pl.when((z >= d) & (z + 1 < n))
            def _():
                up(stream, d).wait_send()

            @pl.when((z + d < n) & (z >= 1))
            def _():
                down(stream, d).wait_send()

    def direct(h, c):
        to = c + 1
        part = held.at[h, z, 2 + c]
        return remote(part, part, s2.at[h, c], r2.at[h, z], band, line(to))

    def direct_start(h):
        for c in range(2):
            @pl.when(z != c + 1)
            def _():
                direct(h, c).start()

    own = jnp.where(z == 0, 0, jnp.where(z == 1, 2, jnp.where(z == 2, 3, 1)))

    def received(h):
        for src in range(n):
            @pl.when((z != src) & ((z == 1) | (z == 2)))
            def _():
                part = held.at[h, src, 2]
                pltpu.make_async_remote_copy(
                    src_ref=part, dst_ref=held.at[h, src, own],
                    send_sem=s2.at[h, 0], recv_sem=r2.at[h, src],
                    device_id=(band, grid), device_id_type=pl.DeviceIdType.MESH,
                ).wait_recv()

    def fourth(h, v, k):
        q, to_band, to_grid = peer(k)
        return remote(packed.at[h, q, v], lines.at[h, me, v], s4.at[h, v, k], r4.at[h, v, k], to_band, to_grid)

    def fourth_local(h, v):
        return pltpu.make_async_copy(packed.at[h, me, v], lines.at[h, me, v], loc.at[2 + v, h])

    def densities(h):
        @pl.loop(0, 2)
        def _(v):
            reals, imags = [], []
            for src in range(n):
                for p in range(PLANES):
                    own_re, own_im = held[h, src, own, 0, p], held[h, src, own, 1, p]
                    vis_re, vis_im = held[h, src, v, 0, p], held[h, src, v, 1, p]
                    reals.append(vis_re * own_re + vis_im * own_im)
                    imags.append(vis_re * own_im - vis_im * own_re)
            pair = jnp.concatenate([jnp.concatenate(reals, axis=0), jnp.concatenate(imags, axis=0)], axis=1)
            value = right(pair, zf_ref)
            for i in range(0, PLANES * n, 2):
                both = [
                    jnp.concatenate([value[p * ny:(p + 1) * ny, :nz], value[p * ny:(p + 1) * ny, nz:]], axis=0)
                    for p in (i, i + 1)
                ]
                done = left(yf_ref, jnp.concatenate(both, axis=1))
                for p in range(2):
                    for part in range(2):
                        piece = done[part * ny:(part + 1) * ny, p * nz:(p + 1) * nz]
                        packed[h, :, v, :, part, i + p, :] = piece.reshape(peers, rows, nz)

            for k in range(1, peers):
                fourth(h, v, k).start()
            fourth_local(h, v).start()

    first_wait(0)
    hop(0, 0)
    first_start(1)
    hop(0, 1)
    screen_local.wait()
    tables_local.wait()
    for h in range(1, ROUNDS):
        first_wait(h)
        hop(h, 0)
        if h + 1 < ROUNDS:
            first_start(h + 1)
        hop(h - 1, 2)
        direct_start(h - 1)
        hop(h, 1)
        hop(h - 1, 3)
        received(h - 1)
        densities(h - 1)
    last = ROUNDS - 1
    hop(last, 2)
    direct_start(last)
    hop(ROUNDS, 0)
    hop(last, 3)
    received(last)
    hop(ROUNDS, 1)
    densities(last)
    for d in range(2, n):
        hop(ROUNDS, d)

    def sixth(h, v, k):
        q, to_band, to_grid = peer(k)
        return remote(packed.at[h, q, v], back.at[h, me, v], s6.at[h, v, k], r6.at[h, v, k], to_band, to_grid)

    def sixth_local(h, v):
        return pltpu.make_async_copy(packed.at[h, me, v], back.at[h, me, v], loc.at[4 + v, h])

    def sixth_start(h, v):
        for k in range(1, peers):
            sixth(h, v, k).start()
        sixth_local(h, v).start()

    def sixth_wait(h, v):
        sixth_local(h, v).wait()
        for k in range(1, peers):
            sixth(h, v, k).wait_recv()

    @pl.loop(0, 2)
    def _(v):
        for h in range(ROUNDS):
            fourth_local(h, v).wait()
            for k in range(1, peers):
                fourth(h, v, k).wait()

        @pl.loop(0, n)
        def _(src):
            for c in range(0, n, 2):
                both = [
                    jnp.concatenate(
                        [lines[:, :, v, src * n + c + p, part].reshape(nx, nz) for part in range(2)], axis=0
                    )
                    for p in range(2)
                ]
                weight = jnp.concatenate([screen[src, c], screen[src, c + 1]], axis=1)
                value = left(xf_ref, jnp.concatenate(both, axis=1))
                value = value * jnp.concatenate([weight, weight], axis=0)
                value = left(xi_ref, value)
                for p in range(2):
                    for part in range(2):
                        piece = value[part * nx:(part + 1) * nx, p * nz:(p + 1) * nz]
                        packed[:, :, v, src * n + c + p, part] = piece.reshape(ROUNDS, peers, n * PLANES, nz)

        sixth_start(0, v)

    def seventh(h, to):
        return remote(result.at[h, to], slab.at[h, z], s7.at[h, to], r7.at[h, z], band, line(to))

    def seventh_local(h, to):
        return pltpu.make_async_copy(result.at[h, to], slab.at[h, to], loc.at[6, h])

    def out_part(j, h):
        return out_ref.at[0, :, pl.ds(j * n + h * PLANES, PLANES)]

    def eighth(h, src):
        return remote(slab.at[h, src], out_part(band, h), s8.at[h, src], r8.at[h, band], PLANE_BAND[src], grid)

    def eighth_local(h, src):
        return pltpu.make_async_copy(slab.at[h, src], out_part(band, h), loc.at[7, h])

    def deliver(h):
        for src in range(n):
            @pl.when(z == src)
            def _():
                seventh_local(h, src).wait()

            @pl.when(z != src)
            def _():
                pltpu.make_async_remote_copy(
                    src_ref=result.at[h, src], dst_ref=slab.at[h, src],
                    send_sem=s7.at[h, src], recv_sem=r7.at[h, src],
                    device_id=(band, grid), device_id_type=pl.DeviceIdType.MESH,
                ).wait_recv()

            @pl.when(band == PLANE_BAND[src])
            def _():
                eighth_local(h, src).start()

            @pl.when(band != PLANE_BAND[src])
            def _():
                eighth(h, src).start()

    for h in range(ROUNDS):
        for v in range(2):
            sixth_wait(h, v)
            if h + 1 < ROUNDS:
                sixth_start(h + 1, v)
        for src in range(n):
            for p in range(PLANES):
                i = src * PLANES + p
                both = [
                    jnp.concatenate([back[h, :, v, :, part, i, :].reshape(ny, nz) for part in range(2)], axis=0)
                    for v in range(2)
                ]
                value = left(yi_ref, jnp.concatenate(both, axis=1))
                value = jnp.concatenate(
                    [
                        jnp.concatenate([value[:ny, v * nz:(v + 1) * nz], value[ny:, v * nz:(v + 1) * nz]], axis=1)
                        for v in range(2)
                    ],
                    axis=0,
                )
                value = -0.25 * right(value, zi_ref)
                total_re, total_im = 0.0, 0.0
                for v in range(2):
                    pot_re, pot_im = value[v * ny:(v + 1) * ny, :nz], value[v * ny:(v + 1) * ny, nz:]
                    vis_re, vis_im = held[h, src, v, 0, p], held[h, src, v, 1, p]
                    total_re = total_re + (pot_re * vis_re - pot_im * vis_im)
                    total_im = total_im + (pot_re * vis_im + pot_im * vis_re)
                result[h, src, 0, p] = total_re
                result[h, src, 1, p] = total_im

            @pl.when(z == src)
            def _():
                seventh_local(h, src).start()

            @pl.when(z != src)
            def _():
                seventh(h, src).start()
        if h > 0:
            deliver(h - 1)
    deliver(last)

    for h in range(ROUNDS):
        for d in range(1, n):
            first(h, d).wait_send()
        for c in range(2):
            @pl.when(z != c + 1)
            def _():
                direct(h, c).wait_send()
        for v in range(2):
            for k in range(1, peers):
                sixth(h, v, k).wait_send()
        for src in range(n):
            @pl.when(z != src)
            def _():
                seventh(h, src).wait_send()

            @pl.when(band == PLANE_BAND[src])
            def _():
                eighth_local(h, src).wait()

            @pl.when(band != PLANE_BAND[src])
            def _():
                eighth(h, src).wait_send()

            @pl.when(band != src)
            def _():
                pltpu.make_async_remote_copy(
                    src_ref=slab.at[h, 0], dst_ref=out_part(src, h),
                    send_sem=s8.at[h, src], recv_sem=r8.at[h, src],
                    device_id=(band, grid), device_id_type=pl.DeviceIdType.MESH,
                ).wait_recv()
    for stream in range(ROUNDS + 1):
        hops_sent(stream, (0, 1, 2))


def fused(bands, coulomb):
    n = GROUPS
    spread = lax.axis_size("grid") // n
    peers = n * spread
    nx, ny, nz = coulomb.shape[0], bands.shape[3], bands.shape[4]
    rows = ny // peers
    q = np.arange(peers)
    row_order = (
        (np.arange(n)[None, :, None] * spread + (q % spread)[:, None, None]) * rows
        + (q // spread)[:, None, None] * n
        + np.arange(n)[None, None, :]
    ).reshape(-1)
    plane_order = (
        np.arange(n)[None, None, :, None] * (nx // n)
        + (q % spread)[None, :, None, None] * (nx // n // spread)
        + (q // spread)[None, :, None, None] * n
        + np.arange(ROUNDS)[:, None, None, None] * PLANES
        + np.arange(PLANES)
    ).reshape(-1)
    tabs = jnp.asarray(np.stack(permuted_tables(nx, 1.0 / (nx * ny * nz), row_order, plane_order)))
    mine = lax.dynamic_slice_in_dim(coulomb, lax.axis_index("band") * n, n, axis=1).transpose(1, 0, 2)
    f32 = jnp.float32
    blocks = (ROUNDS, peers, 2, rows, 2, n * PLANES, nz)
    sem = pltpu.SemaphoreType.DMA
    return pl.pallas_call(
        functools.partial(fused_kernel, spread),
        in_specs=[pl.BlockSpec(memory_space=pl.ANY)] * 3,
        out_specs=pl.BlockSpec(memory_space=pl.ANY),
        out_shape=jax.ShapeDtypeStruct(bands.shape, f32),
        scratch_shapes=[
            pltpu.VMEM(tabs.shape, tabs.dtype),
            pltpu.VMEM((ROUNDS, n, n, 2, PLANES, ny, nz), f32),
            pltpu.VMEM((n, n, nx, nz), f32),
            pltpu.VMEM(blocks, f32),
            pltpu.VMEM(blocks, f32),
            pltpu.VMEM(blocks, f32),
            pltpu.VMEM((ROUNDS, n, 2, PLANES, ny, nz), f32),
            pltpu.VMEM((ROUNDS, n, 2, PLANES, ny, nz), f32),
            sem((ROUNDS, n)), sem((ROUNDS, n)),
            sem((ROUNDS, 2)), sem((ROUNDS, n)),
            sem((ROUNDS + 1, n)), sem((ROUNDS + 1, n)),
            sem((ROUNDS + 1, n)), sem((ROUNDS + 1, n)),
            sem((ROUNDS, 2, peers)), sem((ROUNDS, 2, peers)),
            sem((ROUNDS, 2, peers)), sem((ROUNDS, 2, peers)),
            sem((ROUNDS, n)), sem((ROUNDS, n)),
            sem((ROUNDS, n)), sem((ROUNDS, n)),
            sem((8, ROUNDS)),
        ],
        compiler_params=pltpu.CompilerParams(
            collective_id=0, has_side_effects=True, vmem_limit_bytes=VMEM_LIMIT
        ),
        name="exchange_by_planes",
    )(bands, mine, tabs)


def fits(bands, coulomb):
    groups, shards = lax.axis_size("band"), lax.axis_size("grid")
    return (
        bands.shape[0] == 1
        and groups == GROUPS
        and shards % GROUPS == 0
        and bands.shape[2] == GROUPS * GROUPS
        and bands.shape[3] == GROUPS * GROUPS * shards
        and coulomb.shape[0] == bands.shape[3] == bands.shape[4]
    )


def body(bands, coulomb):
    if fits(bands, coulomb):
        return fused(bands, coulomb)
    return by_pairs(bands, coulomb)


def solution(mesh):
    in_specs = (P("band", None, "grid", None, None), P(None, "grid", None))
    out_specs = P("band", None, "grid", None, None)
    return jax.shard_map(body, mesh=mesh, in_specs=in_specs, out_specs=out_specs, check_vma=False)
```

```python
import functools

import jax
import jax.numpy as jnp
import ml_dtypes
import numpy as np
from jax import lax
from jax.experimental import pallas as pl
from jax.experimental.pallas import tpu as pltpu
from jax.sharding import PartitionSpec as P

STEPS = 2
VMEM_LIMIT = 48 * 1024 * 1024


def split_table(table):
    high = table.astype(ml_dtypes.bfloat16)
    low = (table - high.astype(np.float64)).astype(ml_dtypes.bfloat16)
    return np.stack([high, low])


def tables(length, scale):
    index = np.arange(length)
    angle = (index[:, None] * index[None, :] % length) * (2.0 * np.pi / length)
    cosine, sine = np.cos(angle), np.sin(angle)
    forward = np.block([[cosine, sine], [-sine, cosine]])
    inverse = np.block([[cosine, -sine], [sine, cosine]])
    return [split_table(t) for t in (forward, inverse, inverse * scale, forward.T, inverse.T)]


def split(values):
    high = values.astype(jnp.bfloat16)
    return high, (values - high.astype(jnp.float32)).astype(jnp.bfloat16)


def dot(a, b):
    return jnp.dot(a, b, preferred_element_type=jnp.float32)


def left(table_ref, values):
    high, low = split(values)
    return dot(table_ref[0], high) + (dot(table_ref[1], high) + dot(table_ref[0], low))


def right(values, table_ref):
    high, low = split(values)
    return dot(high, table_ref[0]) + (dot(high, table_ref[1]) + dot(low, table_ref[0]))


def forward_kernel(own_ref, vis_ref, left_ref, right_ref, out_ref):
    planes, ny, nz = own_ref.shape[2:]
    shards, _, rows = out_ref.shape[:3]
    own_re, own_im, vis_re, vis_im = own_ref[0, 0], own_ref[0, 1], vis_ref[0, 0], vis_ref[0, 1]
    real = vis_re * own_re + vis_im * own_im
    imag = vis_re * own_im - vis_im * own_re
    pair = jnp.concatenate([real.reshape(planes * ny, nz), imag.reshape(planes * ny, nz)], axis=1)
    lines = right(pair, right_ref)
    for i in range(0, planes, 2):
        both = [
            jnp.concatenate([lines[p * ny:(p + 1) * ny, :nz], lines[p * ny:(p + 1) * ny, nz:]], axis=0)
            for p in (i, i + 1)
        ]
        result = left(left_ref, jnp.concatenate(both, axis=1))
        for p in range(2):
            for part in range(2):
                piece = result[part * ny:(part + 1) * ny, p * nz:(p + 1) * nz]
                out_ref[:, part, :, i + p, :] = piece.reshape(shards, rows, nz)


def pencil_kernel(in_ref, coulomb_ref, forward_ref, inverse_ref, out_ref):
    shards, _, rows, planes, nz = in_ref.shape
    nx = shards * planes
    for k in range(0, rows, 2):
        both = []
        for q in (k, k + 1):
            both.append(
                jnp.concatenate([in_ref[:, part, q].reshape(nx, nz) for part in range(2)], axis=0)
            )
        weight = jnp.concatenate([coulomb_ref[:, k, :], coulomb_ref[:, k + 1, :]], axis=1)
        value = left(forward_ref, jnp.concatenate(both, axis=1))
        value = value * jnp.concatenate([weight, weight], axis=0)
        value = left(inverse_ref, value)
        for q in range(2):
            for part in range(2):
                piece = value[part * nx:(part + 1) * nx, q * nz:(q + 1) * nz]
                out_ref[:, part, k + q] = piece.reshape(shards, planes, nz)


def inverse_kernel(has_base, in_ref, vis_ref, left_ref, right_ref, *rest):
    base_ref, out_ref = rest if has_base else (None, rest[0])
    shards, _, rows, planes, nz = in_ref.shape
    ny = shards * rows
    for i in range(0, planes, 2):
        both = []
        for p in (i, i + 1):
            both.append(
                jnp.concatenate([in_ref[:, part, :, p, :].reshape(ny, nz) for part in range(2)], axis=0)
            )
        result = left(left_ref, jnp.concatenate(both, axis=1))
        for p in range(2):
            cut = result[:, p * nz:(p + 1) * nz]
            value = right(jnp.concatenate([cut[:ny], cut[ny:]], axis=1), right_ref)
            pot_re, pot_im = -0.25 * value[:, :nz], -0.25 * value[:, nz:]
            vis_re, vis_im = vis_ref[0, 0, i + p], vis_ref[0, 1, i + p]
            out_re = pot_re * vis_re - pot_im * vis_im
            out_im = pot_re * vis_im + pot_im * vis_re
            if has_base:
                out_re = out_re + base_ref[0, 0, i + p]
                out_im = out_im + base_ref[0, 1, i + p]
            out_ref[0, 0, i + p] = out_re
            out_ref[0, 1, i + p] = out_im


def whole_spec(array):
    return pl.BlockSpec(array.shape, lambda i: (0,) * array.ndim)


def forward(own, vis, shards, tabs):
    _, _, planes, ny, nz = own.shape
    step = min(8, planes)
    slab = pl.BlockSpec((1, 2, step, ny, nz), lambda i: (0, 0, i, 0, 0))
    return pl.pallas_call(
        forward_kernel,
        grid=(planes // step,),
        in_specs=[slab, slab, whole_spec(tabs[0]), whole_spec(tabs[3])],
        out_specs=pl.BlockSpec((shards, 2, ny // shards, step, nz), lambda i: (0, 0, 0, i, 0)),
        out_shape=jax.ShapeDtypeStruct((shards, 2, ny // shards, planes, nz), jnp.float32),
        compiler_params=pltpu.CompilerParams(vmem_limit_bytes=VMEM_LIMIT),
        name="pair_density_dft",
    )(own, vis, tabs[0], tabs[3])


def pencil(block, coulomb, tabs):
    shards, _, rows, planes, nz = block.shape
    step = min(8, rows)
    spec = pl.BlockSpec((shards, 2, step, planes, nz), lambda i: (0, 0, i, 0, 0))
    return pl.pallas_call(
        pencil_kernel,
        grid=(rows // step,),
        in_specs=[
            spec,
            pl.BlockSpec((coulomb.shape[0], step, nz), lambda i: (0, i, 0)),
            whole_spec(tabs[0]),
            whole_spec(tabs[2]),
        ],
        out_specs=spec,
        out_shape=jax.ShapeDtypeStruct(block.shape, jnp.float32),
        compiler_params=pltpu.CompilerParams(vmem_limit_bytes=VMEM_LIMIT),
        name="screen_pencils",
    )(block, coulomb, tabs[0], tabs[2])


def inverse(block, vis, base, tabs):
    shards, _, rows, planes, nz = block.shape
    step = min(8, planes)
    slab = pl.BlockSpec((1, 2, step, shards * rows, nz), lambda i: (0, 0, i, 0, 0))
    extra = [] if base is None else [base]
    return pl.pallas_call(
        functools.partial(inverse_kernel, base is not None),
        grid=(planes // step,),
        in_specs=[
            pl.BlockSpec((shards, 2, rows, step, nz), lambda i: (0, 0, 0, i, 0)),
            slab,
            whole_spec(tabs[1]),
            whole_spec(tabs[4]),
        ] + [slab] * len(extra),
        out_specs=slab,
        out_shape=jax.ShapeDtypeStruct(vis.shape, jnp.float32),
        compiler_params=pltpu.CompilerParams(vmem_limit_bytes=VMEM_LIMIT),
        name="potential_to_exchange",
    )(block, vis, tabs[1], tabs[4], *extra)


def by_pairs(bands, coulomb):
    groups = lax.axis_size("band")
    shards = lax.axis_size("grid")
    span = groups // STEPS
    nx, ny, nz = coulomb.shape[0], bands.shape[3], bands.shape[4]
    tabs = [jnp.asarray(t) for t in tables(nx, 1.0 / (nx * ny * nz))]

    place = lax.axis_index("band") % span
    near = bands
    reach = 1
    while reach < span:
        moves = [(s * span + i, s * span + i + reach) for s in range(STEPS) for i in range(min(reach, span - reach))]
        arrived = lax.ppermute(near, "band", moves)
        near = jnp.where((place >= reach) & (place < 2 * reach), arrived, near)
        reach *= 2
    visitors = [near]
    for _ in range(STEPS - 1):
        visitors.append(lax.ppermute(visitors[-1], "band", [(i, (i + span) % groups) for i in range(groups)]))

    total = None
    sent = [forward(bands, vis, shards, tabs) for vis in visitors]
    sent = [lax.all_to_all(s, "grid", 0, 0, tiled=True) for s in sent]
    sent = [pencil(s, coulomb, tabs) for s in sent]
    sent = [lax.all_to_all(s, "grid", 0, 0, tiled=True) for s in sent]
    for block, vis in zip(sent, visitors):
        total = inverse(block, vis, total, tabs)
    return total


def permuted_tables(length, scale, row_order, plane_order):
    index = np.arange(length)
    angle = (index[:, None] * index[None, :] % length) * (2.0 * np.pi / length)
    cosine, sine = np.cos(angle), np.sin(angle)
    forward = np.block([[cosine, sine], [-sine, cosine]])
    inverse = np.block([[cosine, -sine], [sine, cosine]])
    rows = np.concatenate([row_order, row_order + length])
    planes = np.concatenate([plane_order, plane_order + length])
    return [
        forward.T,
        forward[rows],
        forward[:, planes],
        inverse[planes] * scale,
        inverse[:, rows],
        inverse.T,
    ]


GROUPS = 4
ROUNDS = 4
PLANES = GROUPS // ROUNDS
PLANE_BAND = (0, 1, 3, 2)
PLANE_SLOT = (0, 2, 3, 1)


def fused_kernel(
    spread,
    bands_ref, coulomb_ref, tables_ref,
    out_ref,
    whole_tabs, tabs, weights, held, screen, packed, lines, back, result, slab,
    s1, r1, s2, r2, su, ru, sd, rd, s4, r4, s6, r6, s7, r7, s8, r8, loc,
):
    n = GROUPS
    peers = n * spread
    zf_ref, yf_ref, xf_ref, xi_ref, yi_ref, zi_ref = (tabs.at[i] for i in range(6))
    band = lax.axis_index("band")
    grid = lax.axis_index("grid")
    z = grid // spread
    t = grid % spread
    me = band * spread + t
    ny, nz = bands_ref.shape[3], bands_ref.shape[4]
    rows = ny // peers
    nx = peers * n * PLANES * ROUNDS

    def remote(src, dst, send, recv, to_band, to_grid):
        return pltpu.make_async_remote_copy(
            src_ref=src, dst_ref=dst, send_sem=send, recv_sem=recv,
            device_id=(to_band, to_grid), device_id_type=pl.DeviceIdType.MESH,
        )

    def peer(k):
        q = (me + k) % peers
        return q, q // spread, z * spread + q % spread

    def line(k):
        return k * spread + t

    barrier = pltpu.get_barrier_semaphore()
    for k in range(1, peers):
        _, to_band, to_grid = peer(k)
        pl.semaphore_signal(barrier, inc=1, device_id=(to_band, to_grid), device_id_type=pl.DeviceIdType.MESH)
    for k in range(1, n):
        pl.semaphore_signal(
            barrier, inc=1, device_id=(band, line((z + k) % n)), device_id_type=pl.DeviceIdType.MESH
        )
    pl.semaphore_wait(barrier, peers - 1 + n - 1)

    slot = (band % 2) * 2 + band // 2

    def chunk(h, j):
        return bands_ref.at[0, :, pl.ds(j * n + h * PLANES, PLANES)]

    def first(h, d):
        to = (band + d) % n
        return remote(chunk(h, to), held.at[h, z, slot], s1.at[h, d], r1.at[h, d], to, grid)

    def first_local(h):
        return pltpu.make_async_copy(chunk(h, band), held.at[h, z, slot], loc.at[0, h])

    tile = pl.multiple_of((band // 2) * 2 * n, 2 * n)
    weights_local = pltpu.make_async_copy(coulomb_ref.at[:, pl.ds(tile, 2 * n)], weights, loc.at[1, 0])
    tables_local = pltpu.make_async_copy(tables_ref, whole_tabs, loc.at[1, 1])

    def first_start(h):
        for d in (2, 1, 3):
            first(h, d).start()
        first_local(h).start()

    def first_wait(h):
        first_local(h).wait()
        for d in range(1, n):
            first(h, d).wait_recv()

    first_start(0)
    weights_local.start()
    tables_local.start()

    def block(stream, src):
        return held.at[stream, src, pl.ds(0, 2)] if stream < ROUNDS else screen.at[src]

    def up(stream, d):
        return remote(
            block(stream, z - d), block(stream, z - d), su.at[stream, d], ru.at[stream, d], band, line(z + 1)
        )

    def down(stream, d):
        return remote(
            block(stream, z + d), block(stream, z + d), sd.at[stream, d], rd.at[stream, d], band, line(z - 1)
        )

    def hop(stream, d):
        if d > 0:
            @pl.when(z >= d)
            def _():
                pltpu.make_async_remote_copy(
                    src_ref=block(stream, z - d), dst_ref=block(stream, z - d),
                    send_sem=su.at[stream, d], recv_sem=ru.at[stream, d - 1],
                    device_id=(band, grid), device_id_type=pl.DeviceIdType.MESH,
                ).wait_recv()

            @pl.when(z + d < n)
            def _():
                pltpu.make_async_remote_copy(
                    src_ref=block(stream, z + d), dst_ref=block(stream, z + d),
                    send_sem=sd.at[stream, d], recv_sem=rd.at[stream, d - 1],
                    device_id=(band, grid), device_id_type=pl.DeviceIdType.MESH,
                ).wait_recv()
        if d < n - 1:
            @pl.when((z >= d) & (z + 1 < n))
            def _():
                up(stream, d).start()

            @pl.when((z + d < n) & (z >= 1))
            def _():
                down(stream, d).start()

    def hops_sent(stream, distances):
        for d in distances:
            @pl.when((z >= d) & (z + 1 < n))
            def _():
                up(stream, d).wait_send()

            @pl.when((z + d < n) & (z >= 1))
            def _():
                down(stream, d).wait_send()

    def direct(h, c):
        to = c + 1
        part = held.at[h, z, 2 + c]
        return remote(part, part, s2.at[h, c], r2.at[h, z], band, line(to))

    def direct_start(h):
        for c in range(2):
            @pl.when(z != c + 1)
            def _():
                direct(h, c).start()

    own = jnp.where(z == 0, 0, jnp.where(z == 1, 2, jnp.where(z == 2, 3, 1)))

    def received(h):
        for src in range(n):
            @pl.when((z != src) & ((z == 1) | (z == 2)))
            def _():
                part = held.at[h, src, 2]
                pltpu.make_async_remote_copy(
                    src_ref=part, dst_ref=held.at[h, src, own],
                    send_sem=s2.at[h, 0], recv_sem=r2.at[h, src],
                    device_id=(band, grid), device_id_type=pl.DeviceIdType.MESH,
                ).wait_recv()

    def fourth(h, v, k):
        q, to_band, to_grid = peer(k)
        return remote(packed.at[h, q, v], lines.at[h, me, v], s4.at[h, v, k], r4.at[h, v, k], to_band, to_grid)

    def fourth_local(h, v):
        return pltpu.make_async_copy(packed.at[h, me, v], lines.at[h, me, v], loc.at[2 + v, h])

    def densities(h):
        @pl.loop(0, 2)
        def _(v):
            reals, imags = [], []
            for src in range(n):
                for p in range(PLANES):
                    own_re, own_im = held[h, src, own, 0, p], held[h, src, own, 1, p]
                    vis_re, vis_im = held[h, src, v, 0, p], held[h, src, v, 1, p]
                    reals.append(vis_re * own_re + vis_im * own_im)
                    imags.append(vis_re * own_im - vis_im * own_re)
            pair = jnp.concatenate([jnp.concatenate(reals, axis=0), jnp.concatenate(imags, axis=0)], axis=1)
            value = right(pair, zf_ref)
            for i in range(0, PLANES * n, 2):
                both = [
                    jnp.concatenate([value[p * ny:(p + 1) * ny, :nz], value[p * ny:(p + 1) * ny, nz:]], axis=0)
                    for p in (i, i + 1)
                ]
                done = left(yf_ref, jnp.concatenate(both, axis=1))
                for p in range(2):
                    for part in range(2):
                        piece = done[part * ny:(part + 1) * ny, p * nz:(p + 1) * nz]
                        packed[h, :, v, :, part, i + p, :] = piece.reshape(peers, rows, nz)

            for k in range(1, peers):
                fourth(h, v, k).start()
            fourth_local(h, v).start()

    weights_local.wait()
    for c in range(n):
        screen[z, c] = jnp.where(band % 2 == 0, weights[:, c], weights[:, n + c])
    hop(ROUNDS, 0)
    first_wait(0)
    hop(0, 0)
    first_start(1)
    hop(0, 1)
    tables_local.wait()
    for i in range(6):
        tabs[i, 0], tabs[i, 1] = split(whole_tabs[i])
    for h in range(1, ROUNDS):
        first_wait(h)
        hop(h, 0)
        if h + 1 < ROUNDS:
            first_start(h + 1)
        hop(h - 1, 2)
        direct_start(h - 1)
        hop(h, 1)
        hop(h - 1, 3)
        received(h - 1)
        densities(h - 1)
    last = ROUNDS - 1
    hop(last, 2)
    direct_start(last)
    hop(ROUNDS, 1)
    hop(last, 3)
    received(last)
    densities(last)
    for d in range(2, n):
        hop(ROUNDS, d)

    def sixth(h, v, k):
        q, to_band, to_grid = peer(k)
        return remote(packed.at[h, q, v], back.at[h, me, v], s6.at[h, v, k], r6.at[h, v, k], to_band, to_grid)

    def sixth_local(h, v):
        return pltpu.make_async_copy(packed.at[h, me, v], back.at[h, me, v], loc.at[4 + v, h])

    def sixth_start(h, v):
        for k in range(1, peers):
            sixth(h, v, k).start()
        sixth_local(h, v).start()

    def sixth_wait(h, v):
        sixth_local(h, v).wait()
        for k in range(1, peers):
            sixth(h, v, k).wait_recv()

    @pl.loop(0, 2)
    def _(v):
        for h in range(ROUNDS):
            fourth_local(h, v).wait()
            for k in range(1, peers):
                fourth(h, v, k).wait()

        @pl.loop(0, n)
        def _(src):
            for c in range(0, n, 2):
                both = [
                    jnp.concatenate(
                        [lines[:, :, v, src * n + c + p, part].reshape(nx, nz) for part in range(2)], axis=0
                    )
                    for p in range(2)
                ]
                weight = jnp.concatenate([screen[src, c], screen[src, c + 1]], axis=1)
                value = left(xf_ref, jnp.concatenate(both, axis=1))
                value = value * jnp.concatenate([weight, weight], axis=0)
                value = left(xi_ref, value)
                for p in range(2):
                    for part in range(2):
                        piece = value[part * nx:(part + 1) * nx, p * nz:(p + 1) * nz]
                        packed[:, :, v, src * n + c + p, part] = piece.reshape(ROUNDS, peers, n * PLANES, nz)

        sixth_start(0, v)

    def seventh(h, to):
        return remote(result.at[h, to], slab.at[h, z], s7.at[h, to], r7.at[h, z], band, line(to))

    def seventh_local(h, to):
        return pltpu.make_async_copy(result.at[h, to], slab.at[h, to], loc.at[6, h])

    def out_part(j, h):
        return out_ref.at[0, :, pl.ds(j * n + h * PLANES, PLANES)]

    def eighth(h, src):
        return remote(slab.at[h, src], out_part(band, h), s8.at[h, src], r8.at[h, band], PLANE_BAND[src], grid)

    def eighth_local(h, src):
        return pltpu.make_async_copy(slab.at[h, src], out_part(band, h), loc.at[7, h])

    def deliver(h):
        for src in range(n):
            @pl.when(z == src)
            def _():
                seventh_local(h, src).wait()

            @pl.when(z != src)
            def _():
                pltpu.make_async_remote_copy(
                    src_ref=result.at[h, src], dst_ref=slab.at[h, src],
                    send_sem=s7.at[h, src], recv_sem=r7.at[h, src],
                    device_id=(band, grid), device_id_type=pl.DeviceIdType.MESH,
                ).wait_recv()

            @pl.when(band == PLANE_BAND[src])
            def _():
                eighth_local(h, src).start()

            @pl.when(band != PLANE_BAND[src])
            def _():
                eighth(h, src).start()

    for h in range(ROUNDS):
        for v in range(2):
            sixth_wait(h, v)
            if h + 1 < ROUNDS:
                sixth_start(h + 1, v)
        for src in range(n):
            for p in range(PLANES):
                i = src * PLANES + p
                both = [
                    jnp.concatenate([back[h, :, v, :, part, i, :].reshape(ny, nz) for part in range(2)], axis=0)
                    for v in range(2)
                ]
                value = left(yi_ref, jnp.concatenate(both, axis=1))
                value = jnp.concatenate(
                    [
                        jnp.concatenate([value[:ny, v * nz:(v + 1) * nz], value[ny:, v * nz:(v + 1) * nz]], axis=1)
                        for v in range(2)
                    ],
                    axis=0,
                )
                value = -0.25 * right(value, zi_ref)
                total_re, total_im = 0.0, 0.0
                for v in range(2):
                    pot_re, pot_im = value[v * ny:(v + 1) * ny, :nz], value[v * ny:(v + 1) * ny, nz:]
                    vis_re, vis_im = held[h, src, v, 0, p], held[h, src, v, 1, p]
                    total_re = total_re + (pot_re * vis_re - pot_im * vis_im)
                    total_im = total_im + (pot_re * vis_im + pot_im * vis_re)
                result[h, src, 0, p] = total_re
                result[h, src, 1, p] = total_im

            @pl.when(z == src)
            def _():
                seventh_local(h, src).start()

            @pl.when(z != src)
            def _():
                seventh(h, src).start()
        if h > 0:
            deliver(h - 1)
    deliver(last)

    for h in range(ROUNDS):
        for d in range(1, n):
            first(h, d).wait_send()
        for c in range(2):
            @pl.when(z != c + 1)
            def _():
                direct(h, c).wait_send()
        for v in range(2):
            for k in range(1, peers):
                sixth(h, v, k).wait_send()
        for src in range(n):
            @pl.when(z != src)
            def _():
                seventh(h, src).wait_send()

            @pl.when(band == PLANE_BAND[src])
            def _():
                eighth_local(h, src).wait()

            @pl.when(band != PLANE_BAND[src])
            def _():
                eighth(h, src).wait_send()

            @pl.when(band != src)
            def _():
                pltpu.make_async_remote_copy(
                    src_ref=slab.at[h, 0], dst_ref=out_part(src, h),
                    send_sem=s8.at[h, src], recv_sem=r8.at[h, src],
                    device_id=(band, grid), device_id_type=pl.DeviceIdType.MESH,
                ).wait_recv()
    for stream in range(ROUNDS + 1):
        hops_sent(stream, (0, 1, 2))


def fused(bands, coulomb):
    n = GROUPS
    spread = lax.axis_size("grid") // n
    peers = n * spread
    nx, ny, nz = coulomb.shape[0], bands.shape[3], bands.shape[4]
    rows = ny // peers
    q = np.arange(peers)
    row_order = (
        (np.arange(n)[None, :, None] * spread + (q % spread)[:, None, None]) * rows
        + (q // spread)[:, None, None] * n
        + np.arange(n)[None, None, :]
    ).reshape(-1)
    plane_order = (
        np.arange(n)[None, None, :, None] * (nx // n)
        + (q % spread)[None, :, None, None] * (nx // n // spread)
        + (q // spread)[None, :, None, None] * n
        + np.arange(ROUNDS)[:, None, None, None] * PLANES
        + np.arange(PLANES)
    ).reshape(-1)
    tabs = jnp.asarray(
        np.stack(permuted_tables(nx, 1.0 / (nx * ny * nz), row_order, plane_order)).astype(np.float32)
    )
    f32 = jnp.float32
    blocks = (ROUNDS, peers, 2, rows, 2, n * PLANES, nz)
    sem = pltpu.SemaphoreType.DMA
    return pl.pallas_call(
        functools.partial(fused_kernel, spread),
        in_specs=[pl.BlockSpec(memory_space=pltpu.HBM)] * 3,
        out_specs=pl.BlockSpec(memory_space=pl.ANY),
        out_shape=jax.ShapeDtypeStruct(bands.shape, f32),
        scratch_shapes=[
            pltpu.VMEM(tabs.shape, f32),
            pltpu.VMEM(tabs.shape[:1] + (2,) + tabs.shape[1:], jnp.bfloat16),
            pltpu.VMEM((nx, 2 * n, nz), f32),
            pltpu.VMEM((ROUNDS, n, n, 2, PLANES, ny, nz), f32),
            pltpu.VMEM((n, n, nx, nz), f32),
            pltpu.VMEM(blocks, f32),
            pltpu.VMEM(blocks, f32),
            pltpu.VMEM(blocks, f32),
            pltpu.VMEM((ROUNDS, n, 2, PLANES, ny, nz), f32),
            pltpu.VMEM((ROUNDS, n, 2, PLANES, ny, nz), f32),
            sem((ROUNDS, n)), sem((ROUNDS, n)),
            sem((ROUNDS, 2)), sem((ROUNDS, n)),
            sem((ROUNDS + 1, n)), sem((ROUNDS + 1, n)),
            sem((ROUNDS + 1, n)), sem((ROUNDS + 1, n)),
            sem((ROUNDS, 2, peers)), sem((ROUNDS, 2, peers)),
            sem((ROUNDS, 2, peers)), sem((ROUNDS, 2, peers)),
            sem((ROUNDS, n)), sem((ROUNDS, n)),
            sem((ROUNDS, n)), sem((ROUNDS, n)),
            sem((8, ROUNDS)),
        ],
        compiler_params=pltpu.CompilerParams(
            collective_id=0, has_side_effects=True, vmem_limit_bytes=VMEM_LIMIT
        ),
        name="exchange_by_planes",
    )(bands, coulomb, tabs)


def fits(bands, coulomb):
    groups, shards = lax.axis_size("band"), lax.axis_size("grid")
    return (
        bands.shape[0] == 1
        and groups == GROUPS
        and shards % GROUPS == 0
        and bands.shape[2] == GROUPS * GROUPS
        and bands.shape[3] == GROUPS * GROUPS * shards
        and coulomb.shape[0] == bands.shape[3] == bands.shape[4]
    )


def body(bands, coulomb):
    if fits(bands, coulomb):
        return fused(bands, coulomb)
    return by_pairs(bands, coulomb)


def solution(mesh):
    in_specs = (P("band", None, "grid", None, None), P(None, "grid", None))
    out_specs = P("band", None, "grid", None, None)
    return jax.shard_map(body, mesh=mesh, in_specs=in_specs, out_specs=out_specs, check_vma=False)
```

```python
import functools

import jax
import jax.numpy as jnp
import ml_dtypes
import numpy as np
from jax import lax
from jax.experimental import pallas as pl
from jax.experimental.pallas import tpu as pltpu
from jax.sharding import PartitionSpec as P

STEPS = 2
VMEM_LIMIT = 48 * 1024 * 1024


def split_table(table):
    high = table.astype(ml_dtypes.bfloat16)
    low = (table - high.astype(np.float64)).astype(ml_dtypes.bfloat16)
    return np.stack([high, low])


def tables(length, scale):
    index = np.arange(length)
    angle = (index[:, None] * index[None, :] % length) * (2.0 * np.pi / length)
    cosine, sine = np.cos(angle), np.sin(angle)
    forward = np.block([[cosine, sine], [-sine, cosine]])
    inverse = np.block([[cosine, -sine], [sine, cosine]])
    return [split_table(t) for t in (forward, inverse, inverse * scale, forward.T, inverse.T)]


def split(values):
    high = values.astype(jnp.bfloat16)
    return high, (values - high.astype(jnp.float32)).astype(jnp.bfloat16)


def dot(a, b):
    return jnp.dot(a, b, preferred_element_type=jnp.float32)


def left(table_ref, values):
    high, low = split(values)
    return dot(table_ref[0], high) + (dot(table_ref[1], high) + dot(table_ref[0], low))


def right(values, table_ref):
    high, low = split(values)
    return dot(high, table_ref[0]) + (dot(high, table_ref[1]) + dot(low, table_ref[0]))


def forward_kernel(own_ref, vis_ref, left_ref, right_ref, out_ref):
    planes, ny, nz = own_ref.shape[2:]
    shards, _, rows = out_ref.shape[:3]
    own_re, own_im, vis_re, vis_im = own_ref[0, 0], own_ref[0, 1], vis_ref[0, 0], vis_ref[0, 1]
    real = vis_re * own_re + vis_im * own_im
    imag = vis_re * own_im - vis_im * own_re
    pair = jnp.concatenate([real.reshape(planes * ny, nz), imag.reshape(planes * ny, nz)], axis=1)
    lines = right(pair, right_ref)
    for i in range(0, planes, 2):
        both = [
            jnp.concatenate([lines[p * ny:(p + 1) * ny, :nz], lines[p * ny:(p + 1) * ny, nz:]], axis=0)
            for p in (i, i + 1)
        ]
        result = left(left_ref, jnp.concatenate(both, axis=1))
        for p in range(2):
            for part in range(2):
                piece = result[part * ny:(part + 1) * ny, p * nz:(p + 1) * nz]
                out_ref[:, part, :, i + p, :] = piece.reshape(shards, rows, nz)


def pencil_kernel(in_ref, coulomb_ref, forward_ref, inverse_ref, out_ref):
    shards, _, rows, planes, nz = in_ref.shape
    nx = shards * planes
    for k in range(0, rows, 2):
        both = []
        for q in (k, k + 1):
            both.append(
                jnp.concatenate([in_ref[:, part, q].reshape(nx, nz) for part in range(2)], axis=0)
            )
        weight = jnp.concatenate([coulomb_ref[:, k, :], coulomb_ref[:, k + 1, :]], axis=1)
        value = left(forward_ref, jnp.concatenate(both, axis=1))
        value = value * jnp.concatenate([weight, weight], axis=0)
        value = left(inverse_ref, value)
        for q in range(2):
            for part in range(2):
                piece = value[part * nx:(part + 1) * nx, q * nz:(q + 1) * nz]
                out_ref[:, part, k + q] = piece.reshape(shards, planes, nz)


def inverse_kernel(has_base, in_ref, vis_ref, left_ref, right_ref, *rest):
    base_ref, out_ref = rest if has_base else (None, rest[0])
    shards, _, rows, planes, nz = in_ref.shape
    ny = shards * rows
    for i in range(0, planes, 2):
        both = []
        for p in (i, i + 1):
            both.append(
                jnp.concatenate([in_ref[:, part, :, p, :].reshape(ny, nz) for part in range(2)], axis=0)
            )
        result = left(left_ref, jnp.concatenate(both, axis=1))
        for p in range(2):
            cut = result[:, p * nz:(p + 1) * nz]
            value = right(jnp.concatenate([cut[:ny], cut[ny:]], axis=1), right_ref)
            pot_re, pot_im = -0.25 * value[:, :nz], -0.25 * value[:, nz:]
            vis_re, vis_im = vis_ref[0, 0, i + p], vis_ref[0, 1, i + p]
            out_re = pot_re * vis_re - pot_im * vis_im
            out_im = pot_re * vis_im + pot_im * vis_re
            if has_base:
                out_re = out_re + base_ref[0, 0, i + p]
                out_im = out_im + base_ref[0, 1, i + p]
            out_ref[0, 0, i + p] = out_re
            out_ref[0, 1, i + p] = out_im


def whole_spec(array):
    return pl.BlockSpec(array.shape, lambda i: (0,) * array.ndim)


def forward(own, vis, shards, tabs):
    _, _, planes, ny, nz = own.shape
    step = min(8, planes)
    slab = pl.BlockSpec((1, 2, step, ny, nz), lambda i: (0, 0, i, 0, 0))
    return pl.pallas_call(
        forward_kernel,
        grid=(planes // step,),
        in_specs=[slab, slab, whole_spec(tabs[0]), whole_spec(tabs[3])],
        out_specs=pl.BlockSpec((shards, 2, ny // shards, step, nz), lambda i: (0, 0, 0, i, 0)),
        out_shape=jax.ShapeDtypeStruct((shards, 2, ny // shards, planes, nz), jnp.float32),
        compiler_params=pltpu.CompilerParams(vmem_limit_bytes=VMEM_LIMIT),
        name="pair_density_dft",
    )(own, vis, tabs[0], tabs[3])


def pencil(block, coulomb, tabs):
    shards, _, rows, planes, nz = block.shape
    step = min(8, rows)
    spec = pl.BlockSpec((shards, 2, step, planes, nz), lambda i: (0, 0, i, 0, 0))
    return pl.pallas_call(
        pencil_kernel,
        grid=(rows // step,),
        in_specs=[
            spec,
            pl.BlockSpec((coulomb.shape[0], step, nz), lambda i: (0, i, 0)),
            whole_spec(tabs[0]),
            whole_spec(tabs[2]),
        ],
        out_specs=spec,
        out_shape=jax.ShapeDtypeStruct(block.shape, jnp.float32),
        compiler_params=pltpu.CompilerParams(vmem_limit_bytes=VMEM_LIMIT),
        name="screen_pencils",
    )(block, coulomb, tabs[0], tabs[2])


def inverse(block, vis, base, tabs):
    shards, _, rows, planes, nz = block.shape
    step = min(8, planes)
    slab = pl.BlockSpec((1, 2, step, shards * rows, nz), lambda i: (0, 0, i, 0, 0))
    extra = [] if base is None else [base]
    return pl.pallas_call(
        functools.partial(inverse_kernel, base is not None),
        grid=(planes // step,),
        in_specs=[
            pl.BlockSpec((shards, 2, rows, step, nz), lambda i: (0, 0, 0, i, 0)),
            slab,
            whole_spec(tabs[1]),
            whole_spec(tabs[4]),
        ] + [slab] * len(extra),
        out_specs=slab,
        out_shape=jax.ShapeDtypeStruct(vis.shape, jnp.float32),
        compiler_params=pltpu.CompilerParams(vmem_limit_bytes=VMEM_LIMIT),
        name="potential_to_exchange",
    )(block, vis, tabs[1], tabs[4], *extra)


def by_pairs(bands, coulomb):
    groups = lax.axis_size("band")
    shards = lax.axis_size("grid")
    span = groups // STEPS
    nx, ny, nz = coulomb.shape[0], bands.shape[3], bands.shape[4]
    tabs = [jnp.asarray(t) for t in tables(nx, 1.0 / (nx * ny * nz))]

    place = lax.axis_index("band") % span
    near = bands
    reach = 1
    while reach < span:
        moves = [(s * span + i, s * span + i + reach) for s in range(STEPS) for i in range(min(reach, span - reach))]
        arrived = lax.ppermute(near, "band", moves)
        near = jnp.where((place >= reach) & (place < 2 * reach), arrived, near)
        reach *= 2
    visitors = [near]
    for _ in range(STEPS - 1):
        visitors.append(lax.ppermute(visitors[-1], "band", [(i, (i + span) % groups) for i in range(groups)]))

    total = None
    sent = [forward(bands, vis, shards, tabs) for vis in visitors]
    sent = [lax.all_to_all(s, "grid", 0, 0, tiled=True) for s in sent]
    sent = [pencil(s, coulomb, tabs) for s in sent]
    sent = [lax.all_to_all(s, "grid", 0, 0, tiled=True) for s in sent]
    for block, vis in zip(sent, visitors):
        total = inverse(block, vis, total, tabs)
    return total


def permuted_tables(length, scale, row_order, plane_order):
    index = np.arange(length)
    angle = (index[:, None] * index[None, :] % length) * (2.0 * np.pi / length)
    cosine, sine = np.cos(angle), np.sin(angle)
    forward = np.block([[cosine, sine], [-sine, cosine]])
    inverse = np.block([[cosine, -sine], [sine, cosine]])
    rows = np.concatenate([row_order, row_order + length])
    planes = np.concatenate([plane_order, plane_order + length])
    return [
        forward.T,
        forward[rows],
        forward[:, planes],
        inverse[planes] * scale,
        inverse[:, rows],
        inverse.T,
    ]


GROUPS = 4
ROUNDS = 4
PLANES = GROUPS // ROUNDS
PLANE_BAND = (0, 1, 3, 2)
PLANE_SLOT = (0, 2, 3, 1)


def fused_kernel(
    spread,
    bands_ref, coulomb_ref, tables_ref,
    out_ref,
    whole_tabs, tabs, weights, held, screen, packed, lines, back, result, slab,
    s1, r1, s2, r2, su, ru, sd, rd, s4, r4, s6, r6, s7, r7, s8, r8, loc,
):
    n = GROUPS
    peers = n * spread
    zf_ref, yf_ref, xf_ref, xi_ref, yi_ref, zi_ref = (tabs.at[i] for i in range(6))
    band = lax.axis_index("band")
    grid = lax.axis_index("grid")
    z = grid // spread
    t = grid % spread
    me = band * spread + t
    ny, nz = bands_ref.shape[3], bands_ref.shape[4]
    rows = ny // peers
    nx = peers * n * PLANES * ROUNDS

    def remote(src, dst, send, recv, to_band, to_grid):
        return pltpu.make_async_remote_copy(
            src_ref=src, dst_ref=dst, send_sem=send, recv_sem=recv,
            device_id=(to_band, to_grid), device_id_type=pl.DeviceIdType.MESH,
        )

    def peer(k):
        q = (me + k) % peers
        return q, q // spread, z * spread + q % spread

    def line(k):
        return k * spread + t

    barrier = pltpu.get_barrier_semaphore()
    for k in range(1, peers):
        _, to_band, to_grid = peer(k)
        pl.semaphore_signal(barrier, inc=1, device_id=(to_band, to_grid), device_id_type=pl.DeviceIdType.MESH)
    for k in range(1, n):
        pl.semaphore_signal(
            barrier, inc=1, device_id=(band, line((z + k) % n)), device_id_type=pl.DeviceIdType.MESH
        )
    pl.semaphore_wait(barrier, peers - 1 + n - 1)

    slot = (band % 2) * 2 + band // 2

    def chunk(h, j):
        return bands_ref.at[0, :, pl.ds(j * n + h * PLANES, PLANES)]

    def first(h, d):
        to = (band + d) % n
        return remote(chunk(h, to), held.at[h, z, slot], s1.at[h, d], r1.at[h, d], to, grid)

    def first_local(h):
        return pltpu.make_async_copy(chunk(h, band), held.at[h, z, slot], loc.at[0, h])

    tile = pl.multiple_of((band // 2) * 2 * n, 2 * n)
    weights_local = pltpu.make_async_copy(coulomb_ref.at[:, pl.ds(tile, 2 * n)], weights, loc.at[1, 0])
    tables_local = pltpu.make_async_copy(tables_ref, whole_tabs, loc.at[1, 1])

    def first_start(h):
        for d in (2, 1, 3):
            first(h, d).start()
        first_local(h).start()

    def first_wait(h):
        first_local(h).wait()
        for d in range(1, n):
            first(h, d).wait_recv()

    first_start(0)
    weights_local.start()
    tables_local.start()

    def block(stream, src):
        return held.at[stream, src, pl.ds(0, 2)] if stream < ROUNDS else screen.at[src]

    def up(stream, d):
        return remote(
            block(stream, z - d), block(stream, z - d), su.at[stream, d], ru.at[stream, d], band, line(z + 1)
        )

    def down(stream, d):
        return remote(
            block(stream, z + d), block(stream, z + d), sd.at[stream, d], rd.at[stream, d], band, line(z - 1)
        )

    def hop(stream, d):
        if d > 0:
            @pl.when(z >= d)
            def _():
                pltpu.make_async_remote_copy(
                    src_ref=block(stream, z - d), dst_ref=block(stream, z - d),
                    send_sem=su.at[stream, d], recv_sem=ru.at[stream, d - 1],
                    device_id=(band, grid), device_id_type=pl.DeviceIdType.MESH,
                ).wait_recv()

            @pl.when(z + d < n)
            def _():
                pltpu.make_async_remote_copy(
                    src_ref=block(stream, z + d), dst_ref=block(stream, z + d),
                    send_sem=sd.at[stream, d], recv_sem=rd.at[stream, d - 1],
                    device_id=(band, grid), device_id_type=pl.DeviceIdType.MESH,
                ).wait_recv()
        if d < n - 1:
            @pl.when((z >= d) & (z + 1 < n))
            def _():
                up(stream, d).start()

            @pl.when((z + d < n) & (z >= 1))
            def _():
                down(stream, d).start()

    def hops_sent(stream, distances):
        for d in distances:
            @pl.when((z >= d) & (z + 1 < n))
            def _():
                up(stream, d).wait_send()

            @pl.when((z + d < n) & (z >= 1))
            def _():
                down(stream, d).wait_send()

    def direct(h, c):
        to = c + 1
        part = held.at[h, z, 2 + c]
        return remote(part, part, s2.at[h, c], r2.at[h, z], band, line(to))

    def direct_start(h):
        for c in range(2):
            @pl.when(z != c + 1)
            def _():
                direct(h, c).start()

    own = jnp.where(z == 0, 0, jnp.where(z == 1, 2, jnp.where(z == 2, 3, 1)))

    def received(h):
        for src in range(n):
            @pl.when((z != src) & ((z == 1) | (z == 2)))
            def _():
                part = held.at[h, src, 2]
                pltpu.make_async_remote_copy(
                    src_ref=part, dst_ref=held.at[h, src, own],
                    send_sem=s2.at[h, 0], recv_sem=r2.at[h, src],
                    device_id=(band, grid), device_id_type=pl.DeviceIdType.MESH,
                ).wait_recv()

    def fourth(h, v, k):
        q, to_band, to_grid = peer(k)
        return remote(packed.at[h, q, v], lines.at[h, me, v], s4.at[h, v, k], r4.at[h, v, k], to_band, to_grid)

    def fourth_local(h, v):
        return pltpu.make_async_copy(packed.at[h, me, v], lines.at[h, me, v], loc.at[2 + v, h])

    def densities(h):
        @pl.loop(0, 2)
        def _(v):
            reals, imags = [], []
            for src in range(n):
                for p in range(PLANES):
                    own_re, own_im = held[h, src, own, 0, p], held[h, src, own, 1, p]
                    vis_re, vis_im = held[h, src, v, 0, p], held[h, src, v, 1, p]
                    reals.append(vis_re * own_re + vis_im * own_im)
                    imags.append(vis_re * own_im - vis_im * own_re)
            pair = jnp.concatenate([jnp.concatenate(reals, axis=0), jnp.concatenate(imags, axis=0)], axis=1)
            value = right(pair, zf_ref)
            for i in range(0, PLANES * n, 2):
                both = [
                    jnp.concatenate([value[p * ny:(p + 1) * ny, :nz], value[p * ny:(p + 1) * ny, nz:]], axis=0)
                    for p in (i, i + 1)
                ]
                done = left(yf_ref, jnp.concatenate(both, axis=1))
                for p in range(2):
                    for part in range(2):
                        piece = done[part * ny:(part + 1) * ny, p * nz:(p + 1) * nz]
                        packed[h, :, v, :, part, i + p, :] = piece.reshape(peers, rows, nz)

            for k in range(1, peers):
                fourth(h, v, k).start()
            fourth_local(h, v).start()

    weights_local.wait()
    for c in range(n):
        screen[z, c] = jnp.where(band % 2 == 0, weights[:, c], weights[:, n + c])
    hop(ROUNDS, 0)
    first_wait(0)
    hop(0, 0)
    first_start(1)
    hop(0, 1)
    tables_local.wait()
    for i in range(6):
        tabs[i, 0], tabs[i, 1] = split(whole_tabs[i])
    for h in range(1, ROUNDS):
        first_wait(h)
        hop(h, 0)
        if h + 1 < ROUNDS:
            first_start(h + 1)
        hop(h - 1, 2)
        direct_start(h - 1)
        hop(h, 1)
        if h > 1:
            hop(h - 2, 3)
            received(h - 2)
            densities(h - 2)
    last = ROUNDS - 1
    hop(last, 2)
    direct_start(last)
    hop(ROUNDS, 1)
    hop(last - 1, 3)
    received(last - 1)
    densities(last - 1)
    hop(last, 3)
    received(last)
    densities(last)
    for d in range(2, n):
        hop(ROUNDS, d)

    def sixth(h, v, k):
        q, to_band, to_grid = peer(k)
        return remote(packed.at[h, q, v], back.at[h, me, v], s6.at[h, v, k], r6.at[h, v, k], to_band, to_grid)

    def sixth_local(h, v):
        return pltpu.make_async_copy(packed.at[h, me, v], back.at[h, me, v], loc.at[4 + v, h])

    def sixth_start(h, v):
        for k in range(1, peers):
            sixth(h, v, k).start()
        sixth_local(h, v).start()

    def sixth_wait(h, v):
        sixth_local(h, v).wait()
        for k in range(1, peers):
            sixth(h, v, k).wait_recv()

    @pl.loop(0, 2)
    def _(v):
        for h in range(ROUNDS):
            fourth_local(h, v).wait()
            for k in range(1, peers):
                fourth(h, v, k).wait()

        @pl.loop(0, n)
        def _(src):
            for c in range(0, n, 2):
                both = [
                    jnp.concatenate(
                        [lines[:, :, v, src * n + c + p, part].reshape(nx, nz) for part in range(2)], axis=0
                    )
                    for p in range(2)
                ]
                weight = jnp.concatenate([screen[src, c], screen[src, c + 1]], axis=1)
                value = left(xf_ref, jnp.concatenate(both, axis=1))
                value = value * jnp.concatenate([weight, weight], axis=0)
                value = left(xi_ref, value)
                for p in range(2):
                    for part in range(2):
                        piece = value[part * nx:(part + 1) * nx, p * nz:(p + 1) * nz]
                        packed[:, :, v, src * n + c + p, part] = piece.reshape(ROUNDS, peers, n * PLANES, nz)

        sixth_start(0, v)

    def seventh(h, to):
        return remote(result.at[h, to], slab.at[h, z], s7.at[h, to], r7.at[h, z], band, line(to))

    def seventh_local(h, to):
        return pltpu.make_async_copy(result.at[h, to], slab.at[h, to], loc.at[6, h])

    def out_part(j, h):
        return out_ref.at[0, :, pl.ds(j * n + h * PLANES, PLANES)]

    def eighth(h, src):
        return remote(slab.at[h, src], out_part(band, h), s8.at[h, src], r8.at[h, band], PLANE_BAND[src], grid)

    def eighth_local(h, src):
        return pltpu.make_async_copy(slab.at[h, src], out_part(band, h), loc.at[7, h])

    def deliver(h):
        for src in range(n):
            @pl.when(z == src)
            def _():
                seventh_local(h, src).wait()

            @pl.when(z != src)
            def _():
                pltpu.make_async_remote_copy(
                    src_ref=result.at[h, src], dst_ref=slab.at[h, src],
                    send_sem=s7.at[h, src], recv_sem=r7.at[h, src],
                    device_id=(band, grid), device_id_type=pl.DeviceIdType.MESH,
                ).wait_recv()

            @pl.when(band == PLANE_BAND[src])
            def _():
                eighth_local(h, src).start()

            @pl.when(band != PLANE_BAND[src])
            def _():
                eighth(h, src).start()

    for h in range(ROUNDS):
        for v in range(2):
            sixth_wait(h, v)
            if h + 1 < ROUNDS:
                sixth_start(h + 1, v)
        for src in range(n):
            for p in range(PLANES):
                i = src * PLANES + p
                both = [
                    jnp.concatenate([back[h, :, v, :, part, i, :].reshape(ny, nz) for part in range(2)], axis=0)
                    for v in range(2)
                ]
                value = left(yi_ref, jnp.concatenate(both, axis=1))
                value = jnp.concatenate(
                    [
                        jnp.concatenate([value[:ny, v * nz:(v + 1) * nz], value[ny:, v * nz:(v + 1) * nz]], axis=1)
                        for v in range(2)
                    ],
                    axis=0,
                )
                value = -0.25 * right(value, zi_ref)
                total_re, total_im = 0.0, 0.0
                for v in range(2):
                    pot_re, pot_im = value[v * ny:(v + 1) * ny, :nz], value[v * ny:(v + 1) * ny, nz:]
                    vis_re, vis_im = held[h, src, v, 0, p], held[h, src, v, 1, p]
                    total_re = total_re + (pot_re * vis_re - pot_im * vis_im)
                    total_im = total_im + (pot_re * vis_im + pot_im * vis_re)
                result[h, src, 0, p] = total_re
                result[h, src, 1, p] = total_im

            @pl.when(z == src)
            def _():
                seventh_local(h, src).start()

            @pl.when(z != src)
            def _():
                seventh(h, src).start()
        if h > 1:
            deliver(h - 2)
    deliver(last - 1)
    deliver(last)

    for h in range(ROUNDS):
        for d in range(1, n):
            first(h, d).wait_send()
        for c in range(2):
            @pl.when(z != c + 1)
            def _():
                direct(h, c).wait_send()
        for v in range(2):
            for k in range(1, peers):
                sixth(h, v, k).wait_send()
        for src in range(n):
            @pl.when(z != src)
            def _():
                seventh(h, src).wait_send()

            @pl.when(band == PLANE_BAND[src])
            def _():
                eighth_local(h, src).wait()

            @pl.when(band != PLANE_BAND[src])
            def _():
                eighth(h, src).wait_send()

            @pl.when(band != src)
            def _():
                pltpu.make_async_remote_copy(
                    src_ref=slab.at[h, 0], dst_ref=out_part(src, h),
                    send_sem=s8.at[h, src], recv_sem=r8.at[h, src],
                    device_id=(band, grid), device_id_type=pl.DeviceIdType.MESH,
                ).wait_recv()
    for stream in range(ROUNDS + 1):
        hops_sent(stream, (0, 1, 2))


def fused(bands, coulomb):
    n = GROUPS
    spread = lax.axis_size("grid") // n
    peers = n * spread
    nx, ny, nz = coulomb.shape[0], bands.shape[3], bands.shape[4]
    rows = ny // peers
    q = np.arange(peers)
    row_order = (
        (np.arange(n)[None, :, None] * spread + (q % spread)[:, None, None]) * rows
        + (q // spread)[:, None, None] * n
        + np.arange(n)[None, None, :]
    ).reshape(-1)
    plane_order = (
        np.arange(n)[None, None, :, None] * (nx // n)
        + (q % spread)[None, :, None, None] * (nx // n // spread)
        + (q // spread)[None, :, None, None] * n
        + np.arange(ROUNDS)[:, None, None, None] * PLANES
        + np.arange(PLANES)
    ).reshape(-1)
    tabs = jnp.asarray(
        np.stack(permuted_tables(nx, 1.0 / (nx * ny * nz), row_order, plane_order)).astype(np.float32)
    )
    f32 = jnp.float32
    blocks = (ROUNDS, peers, 2, rows, 2, n * PLANES, nz)
    sem = pltpu.SemaphoreType.DMA
    return pl.pallas_call(
        functools.partial(fused_kernel, spread),
        in_specs=[pl.BlockSpec(memory_space=pltpu.HBM)] * 3,
        out_specs=pl.BlockSpec(memory_space=pl.ANY),
        out_shape=jax.ShapeDtypeStruct(bands.shape, f32),
        scratch_shapes=[
            pltpu.VMEM(tabs.shape, f32),
            pltpu.VMEM(tabs.shape[:1] + (2,) + tabs.shape[1:], jnp.bfloat16),
            pltpu.VMEM((nx, 2 * n, nz), f32),
            pltpu.VMEM((ROUNDS, n, n, 2, PLANES, ny, nz), f32),
            pltpu.VMEM((n, n, nx, nz), f32),
            pltpu.VMEM(blocks, f32),
            pltpu.VMEM(blocks, f32),
            pltpu.VMEM(blocks, f32),
            pltpu.VMEM((ROUNDS, n, 2, PLANES, ny, nz), f32),
            pltpu.VMEM((ROUNDS, n, 2, PLANES, ny, nz), f32),
            sem((ROUNDS, n)), sem((ROUNDS, n)),
            sem((ROUNDS, 2)), sem((ROUNDS, n)),
            sem((ROUNDS + 1, n)), sem((ROUNDS + 1, n)),
            sem((ROUNDS + 1, n)), sem((ROUNDS + 1, n)),
            sem((ROUNDS, 2, peers)), sem((ROUNDS, 2, peers)),
            sem((ROUNDS, 2, peers)), sem((ROUNDS, 2, peers)),
            sem((ROUNDS, n)), sem((ROUNDS, n)),
            sem((ROUNDS, n)), sem((ROUNDS, n)),
            sem((8, ROUNDS)),
        ],
        compiler_params=pltpu.CompilerParams(
            collective_id=0, has_side_effects=True, vmem_limit_bytes=VMEM_LIMIT
        ),
        name="exchange_by_planes",
    )(bands, coulomb, tabs)


def fits(bands, coulomb):
    groups, shards = lax.axis_size("band"), lax.axis_size("grid")
    return (
        bands.shape[0] == 1
        and groups == GROUPS
        and shards % GROUPS == 0
        and bands.shape[2] == GROUPS * GROUPS
        and bands.shape[3] == GROUPS * GROUPS * shards
        and coulomb.shape[0] == bands.shape[3] == bands.shape[4]
    )


def body(bands, coulomb):
    if fits(bands, coulomb):
        return fused(bands, coulomb)
    return by_pairs(bands, coulomb)


def solution(mesh):
    in_specs = (P("band", None, "grid", None, None), P(None, "grid", None))
    out_specs = P("band", None, "grid", None, None)
    return jax.shard_map(body, mesh=mesh, in_specs=in_specs, out_specs=out_specs, check_vma=False)
```

```python
import functools

import jax
import jax.numpy as jnp
import ml_dtypes
import numpy as np
from jax import lax
from jax.experimental import pallas as pl
from jax.experimental.pallas import tpu as pltpu
from jax.sharding import PartitionSpec as P

STEPS = 2
VMEM_LIMIT = 48 * 1024 * 1024


def split_table(table):
    high = table.astype(ml_dtypes.bfloat16)
    low = (table - high.astype(np.float64)).astype(ml_dtypes.bfloat16)
    return np.stack([high, low])


def tables(length, scale):
    index = np.arange(length)
    angle = (index[:, None] * index[None, :] % length) * (2.0 * np.pi / length)
    cosine, sine = np.cos(angle), np.sin(angle)
    forward = np.block([[cosine, sine], [-sine, cosine]])
    inverse = np.block([[cosine, -sine], [sine, cosine]])
    return [split_table(t) for t in (forward, inverse, inverse * scale, forward.T, inverse.T)]


def split(values):
    high = values.astype(jnp.bfloat16)
    return high, (values - high.astype(jnp.float32)).astype(jnp.bfloat16)


def dot(a, b):
    return jnp.dot(a, b, preferred_element_type=jnp.float32)


def left(table_ref, values):
    high, low = split(values)
    return dot(table_ref[0], high) + (dot(table_ref[1], high) + dot(table_ref[0], low))


def right(values, table_ref):
    high, low = split(values)
    return dot(high, table_ref[0]) + (dot(high, table_ref[1]) + dot(low, table_ref[0]))


def forward_kernel(own_ref, vis_ref, left_ref, right_ref, out_ref):
    planes, ny, nz = own_ref.shape[2:]
    shards, _, rows = out_ref.shape[:3]
    own_re, own_im, vis_re, vis_im = own_ref[0, 0], own_ref[0, 1], vis_ref[0, 0], vis_ref[0, 1]
    real = vis_re * own_re + vis_im * own_im
    imag = vis_re * own_im - vis_im * own_re
    pair = jnp.concatenate([real.reshape(planes * ny, nz), imag.reshape(planes * ny, nz)], axis=1)
    lines = right(pair, right_ref)
    for i in range(0, planes, 2):
        both = [
            jnp.concatenate([lines[p * ny:(p + 1) * ny, :nz], lines[p * ny:(p + 1) * ny, nz:]], axis=0)
            for p in (i, i + 1)
        ]
        result = left(left_ref, jnp.concatenate(both, axis=1))
        for p in range(2):
            for part in range(2):
                piece = result[part * ny:(part + 1) * ny, p * nz:(p + 1) * nz]
                out_ref[:, part, :, i + p, :] = piece.reshape(shards, rows, nz)


def pencil_kernel(in_ref, coulomb_ref, forward_ref, inverse_ref, out_ref):
    shards, _, rows, planes, nz = in_ref.shape
    nx = shards * planes
    for k in range(0, rows, 2):
        both = []
        for q in (k, k + 1):
            both.append(
                jnp.concatenate([in_ref[:, part, q].reshape(nx, nz) for part in range(2)], axis=0)
            )
        weight = jnp.concatenate([coulomb_ref[:, k, :], coulomb_ref[:, k + 1, :]], axis=1)
        value = left(forward_ref, jnp.concatenate(both, axis=1))
        value = value * jnp.concatenate([weight, weight], axis=0)
        value = left(inverse_ref, value)
        for q in range(2):
            for part in range(2):
                piece = value[part * nx:(part + 1) * nx, q * nz:(q + 1) * nz]
                out_ref[:, part, k + q] = piece.reshape(shards, planes, nz)


def inverse_kernel(has_base, in_ref, vis_ref, left_ref, right_ref, *rest):
    base_ref, out_ref = rest if has_base else (None, rest[0])
    shards, _, rows, planes, nz = in_ref.shape
    ny = shards * rows
    for i in range(0, planes, 2):
        both = []
        for p in (i, i + 1):
            both.append(
                jnp.concatenate([in_ref[:, part, :, p, :].reshape(ny, nz) for part in range(2)], axis=0)
            )
        result = left(left_ref, jnp.concatenate(both, axis=1))
        for p in range(2):
            cut = result[:, p * nz:(p + 1) * nz]
            value = right(jnp.concatenate([cut[:ny], cut[ny:]], axis=1), right_ref)
            pot_re, pot_im = -0.25 * value[:, :nz], -0.25 * value[:, nz:]
            vis_re, vis_im = vis_ref[0, 0, i + p], vis_ref[0, 1, i + p]
            out_re = pot_re * vis_re - pot_im * vis_im
            out_im = pot_re * vis_im + pot_im * vis_re
            if has_base:
                out_re = out_re + base_ref[0, 0, i + p]
                out_im = out_im + base_ref[0, 1, i + p]
            out_ref[0, 0, i + p] = out_re
            out_ref[0, 1, i + p] = out_im


def whole_spec(array):
    return pl.BlockSpec(array.shape, lambda i: (0,) * array.ndim)


def forward(own, vis, shards, tabs):
    _, _, planes, ny, nz = own.shape
    step = min(8, planes)
    slab = pl.BlockSpec((1, 2, step, ny, nz), lambda i: (0, 0, i, 0, 0))
    return pl.pallas_call(
        forward_kernel,
        grid=(planes // step,),
        in_specs=[slab, slab, whole_spec(tabs[0]), whole_spec(tabs[3])],
        out_specs=pl.BlockSpec((shards, 2, ny // shards, step, nz), lambda i: (0, 0, 0, i, 0)),
        out_shape=jax.ShapeDtypeStruct((shards, 2, ny // shards, planes, nz), jnp.float32),
        compiler_params=pltpu.CompilerParams(vmem_limit_bytes=VMEM_LIMIT),
        name="pair_density_dft",
    )(own, vis, tabs[0], tabs[3])


def pencil(block, coulomb, tabs):
    shards, _, rows, planes, nz = block.shape
    step = min(8, rows)
    spec = pl.BlockSpec((shards, 2, step, planes, nz), lambda i: (0, 0, i, 0, 0))
    return pl.pallas_call(
        pencil_kernel,
        grid=(rows // step,),
        in_specs=[
            spec,
            pl.BlockSpec((coulomb.shape[0], step, nz), lambda i: (0, i, 0)),
            whole_spec(tabs[0]),
            whole_spec(tabs[2]),
        ],
        out_specs=spec,
        out_shape=jax.ShapeDtypeStruct(block.shape, jnp.float32),
        compiler_params=pltpu.CompilerParams(vmem_limit_bytes=VMEM_LIMIT),
        name="screen_pencils",
    )(block, coulomb, tabs[0], tabs[2])


def inverse(block, vis, base, tabs):
    shards, _, rows, planes, nz = block.shape
    step = min(8, planes)
    slab = pl.BlockSpec((1, 2, step, shards * rows, nz), lambda i: (0, 0, i, 0, 0))
    extra = [] if base is None else [base]
    return pl.pallas_call(
        functools.partial(inverse_kernel, base is not None),
        grid=(planes // step,),
        in_specs=[
            pl.BlockSpec((shards, 2, rows, step, nz), lambda i: (0, 0, 0, i, 0)),
            slab,
            whole_spec(tabs[1]),
            whole_spec(tabs[4]),
        ] + [slab] * len(extra),
        out_specs=slab,
        out_shape=jax.ShapeDtypeStruct(vis.shape, jnp.float32),
        compiler_params=pltpu.CompilerParams(vmem_limit_bytes=VMEM_LIMIT),
        name="potential_to_exchange",
    )(block, vis, tabs[1], tabs[4], *extra)


def by_pairs(bands, coulomb):
    groups = lax.axis_size("band")
    shards = lax.axis_size("grid")
    span = groups // STEPS
    nx, ny, nz = coulomb.shape[0], bands.shape[3], bands.shape[4]
    tabs = [jnp.asarray(t) for t in tables(nx, 1.0 / (nx * ny * nz))]

    place = lax.axis_index("band") % span
    near = bands
    reach = 1
    while reach < span:
        moves = [(s * span + i, s * span + i + reach) for s in range(STEPS) for i in range(min(reach, span - reach))]
        arrived = lax.ppermute(near, "band", moves)
        near = jnp.where((place >= reach) & (place < 2 * reach), arrived, near)
        reach *= 2
    visitors = [near]
    for _ in range(STEPS - 1):
        visitors.append(lax.ppermute(visitors[-1], "band", [(i, (i + span) % groups) for i in range(groups)]))

    total = None
    sent = [forward(bands, vis, shards, tabs) for vis in visitors]
    sent = [lax.all_to_all(s, "grid", 0, 0, tiled=True) for s in sent]
    sent = [pencil(s, coulomb, tabs) for s in sent]
    sent = [lax.all_to_all(s, "grid", 0, 0, tiled=True) for s in sent]
    for block, vis in zip(sent, visitors):
        total = inverse(block, vis, total, tabs)
    return total


def permuted_tables(length, scale, row_order, plane_order):
    index = np.arange(length)
    angle = (index[:, None] * index[None, :] % length) * (2.0 * np.pi / length)
    cosine, sine = np.cos(angle), np.sin(angle)
    forward = np.block([[cosine, sine], [-sine, cosine]])
    inverse = np.block([[cosine, -sine], [sine, cosine]])
    rows = np.concatenate([row_order, row_order + length])
    planes = np.concatenate([plane_order, plane_order + length])
    return [
        forward.T,
        forward[rows],
        forward[:, planes],
        inverse[planes] * scale,
        inverse[:, rows],
        inverse.T,
    ]


GROUPS = 4
ROUNDS = 4
PLANES = GROUPS // ROUNDS
PLANE_BAND = (0, 1, 3, 2)
PLANE_SLOT = (0, 2, 3, 1)


def fused_kernel(
    spread,
    bands_ref, coulomb_ref, tables_ref,
    out_ref,
    whole_tabs, tabs, weights, held, screen, packed, lines, back, result, slab,
    s1, r1, s2, r2, su, ru, sd, rd, s4, r4, s6, r6, s7, r7, s8, r8, loc,
):
    n = GROUPS
    peers = n * spread
    zf_ref, yf_ref, xf_ref, xi_ref, yi_ref, zi_ref = (tabs.at[i] for i in range(6))
    band = lax.axis_index("band")
    grid = lax.axis_index("grid")
    z = grid // spread
    t = grid % spread
    me = band * spread + t
    ny, nz = bands_ref.shape[3], bands_ref.shape[4]
    rows = ny // peers
    nx = peers * n * PLANES * ROUNDS

    def remote(src, dst, send, recv, to_band, to_grid):
        return pltpu.make_async_remote_copy(
            src_ref=src, dst_ref=dst, send_sem=send, recv_sem=recv,
            device_id=(to_band, to_grid), device_id_type=pl.DeviceIdType.MESH,
        )

    def peer(k):
        q = (me + k) % peers
        return q, q // spread, z * spread + q % spread

    def line(k):
        return k * spread + t

    barrier = pltpu.get_barrier_semaphore()
    for k in range(1, peers):
        _, to_band, to_grid = peer(k)
        pl.semaphore_signal(barrier, inc=1, device_id=(to_band, to_grid), device_id_type=pl.DeviceIdType.MESH)
    for k in range(1, n):
        pl.semaphore_signal(
            barrier, inc=1, device_id=(band, line((z + k) % n)), device_id_type=pl.DeviceIdType.MESH
        )
    pl.semaphore_wait(barrier, peers - 1 + n - 1)

    slot = (band % 2) * 2 + band // 2

    def chunk(h, j):
        return bands_ref.at[0, :, pl.ds(j * n + h * PLANES, PLANES)]

    def first(h, d):
        to = (band + d) % n
        return remote(chunk(h, to), held.at[h, z, slot], s1.at[h, d], r1.at[h, d], to, grid)

    def first_local(h):
        return pltpu.make_async_copy(chunk(h, band), held.at[h, z, slot], loc.at[0, h])

    tile = pl.multiple_of((band // 2) * 2 * n, 2 * n)
    weights_local = pltpu.make_async_copy(coulomb_ref.at[:, pl.ds(tile, 2 * n)], weights, loc.at[1, 0])
    tables_local = pltpu.make_async_copy(tables_ref, whole_tabs, loc.at[1, 1])

    def first_start(h):
        for d in (2, 1, 3):
            first(h, d).start()
        first_local(h).start()

    def first_wait(h):
        first_local(h).wait()
        for d in range(1, n):
            first(h, d).wait_recv()

    first_start(0)
    weights_local.start()
    tables_local.start()

    def block(stream, src):
        return held.at[stream, src, pl.ds(0, 2)] if stream < ROUNDS else screen.at[src]

    def up(stream, d):
        return remote(
            block(stream, z - d), block(stream, z - d), su.at[stream, d], ru.at[stream, d], band, line(z + 1)
        )

    def down(stream, d):
        return remote(
            block(stream, z + d), block(stream, z + d), sd.at[stream, d], rd.at[stream, d], band, line(z - 1)
        )

    def hop(stream, d):
        if d > 0:
            @pl.when(z >= d)
            def _():
                pltpu.make_async_remote_copy(
                    src_ref=block(stream, z - d), dst_ref=block(stream, z - d),
                    send_sem=su.at[stream, d], recv_sem=ru.at[stream, d - 1],
                    device_id=(band, grid), device_id_type=pl.DeviceIdType.MESH,
                ).wait_recv()

            @pl.when(z + d < n)
            def _():
                pltpu.make_async_remote_copy(
                    src_ref=block(stream, z + d), dst_ref=block(stream, z + d),
                    send_sem=sd.at[stream, d], recv_sem=rd.at[stream, d - 1],
                    device_id=(band, grid), device_id_type=pl.DeviceIdType.MESH,
                ).wait_recv()
        if d < n - 1:
            @pl.when((z >= d) & (z + 1 < n))
            def _():
                up(stream, d).start()

            @pl.when((z + d < n) & (z >= 1))
            def _():
                down(stream, d).start()

    def hops_sent(stream, distances):
        for d in distances:
            @pl.when((z >= d) & (z + 1 < n))
            def _():
                up(stream, d).wait_send()

            @pl.when((z + d < n) & (z >= 1))
            def _():
                down(stream, d).wait_send()

    def direct(h, c):
        to = c + 1
        part = held.at[h, z, 2 + c]
        return remote(part, part, s2.at[h, c], r2.at[h, z], band, line(to))

    def direct_start(h):
        for c in range(2):
            @pl.when(z != c + 1)
            def _():
                direct(h, c).start()

    own = jnp.where(z == 0, 0, jnp.where(z == 1, 2, jnp.where(z == 2, 3, 1)))

    def received(h):
        for src in range(n):
            @pl.when((z != src) & ((z == 1) | (z == 2)))
            def _():
                part = held.at[h, src, 2]
                pltpu.make_async_remote_copy(
                    src_ref=part, dst_ref=held.at[h, src, own],
                    send_sem=s2.at[h, 0], recv_sem=r2.at[h, src],
                    device_id=(band, grid), device_id_type=pl.DeviceIdType.MESH,
                ).wait_recv()

    def fourth(h, v, k):
        q, to_band, to_grid = peer(k)
        return remote(packed.at[h, q, v], lines.at[h, me, v], s4.at[h, v, k], r4.at[h, v, k], to_band, to_grid)

    def fourth_local(h, v):
        return pltpu.make_async_copy(packed.at[h, me, v], lines.at[h, me, v], loc.at[2 + v, h])

    def densities(h):
        @pl.loop(0, 2)
        def _(v):
            reals, imags = [], []
            for src in range(n):
                for p in range(PLANES):
                    own_re, own_im = held[h, src, own, 0, p], held[h, src, own, 1, p]
                    vis_re, vis_im = held[h, src, v, 0, p], held[h, src, v, 1, p]
                    reals.append(vis_re * own_re + vis_im * own_im)
                    imags.append(vis_re * own_im - vis_im * own_re)
            pair = jnp.concatenate([jnp.concatenate(reals, axis=0), jnp.concatenate(imags, axis=0)], axis=1)
            value = right(pair, zf_ref)
            for i in range(0, PLANES * n, 2):
                both = [
                    jnp.concatenate([value[p * ny:(p + 1) * ny, :nz], value[p * ny:(p + 1) * ny, nz:]], axis=0)
                    for p in (i, i + 1)
                ]
                done = left(yf_ref, jnp.concatenate(both, axis=1))
                for p in range(2):
                    for part in range(2):
                        piece = done[part * ny:(part + 1) * ny, p * nz:(p + 1) * nz]
                        packed[h, :, v, :, part, i + p, :] = piece.reshape(peers, rows, nz)

            for k in range(1, peers):
                fourth(h, v, k).start()
            fourth_local(h, v).start()

    weights_local.wait()
    for c in range(n):
        screen[z, c] = jnp.where(band % 2 == 0, weights[:, c], weights[:, n + c])
    hop(ROUNDS, 0)
    first_wait(0)
    hop(0, 0)
    first_start(1)
    hop(0, 1)
    tables_local.wait()
    for i in range(6):
        tabs[i, 0], tabs[i, 1] = split(whole_tabs[i])
    for h in range(1, ROUNDS):
        first_wait(h)
        hop(h, 0)
        if h + 1 < ROUNDS:
            first_start(h + 1)
        hop(h - 1, 2)
        direct_start(h - 1)
        hop(h, 1)
        hop(h - 1, 3)
        received(h - 1)
        densities(h - 1)
    last = ROUNDS - 1
    hop(last, 2)
    direct_start(last)
    hop(ROUNDS, 1)
    hop(last, 3)
    received(last)
    densities(last)
    for d in range(2, n):
        hop(ROUNDS, d)

    def sixth(h, v, k):
        q, to_band, to_grid = peer(k)
        return remote(packed.at[h, q, v], back.at[h, me, v], s6.at[h, v, k], r6.at[h, v, k], to_band, to_grid)

    def sixth_local(h, v):
        return pltpu.make_async_copy(packed.at[h, me, v], back.at[h, me, v], loc.at[4 + v, h])

    def sixth_start(h, v):
        for k in range(1, peers):
            sixth(h, v, k).start()
        sixth_local(h, v).start()

    def sixth_wait(h, v):
        sixth_local(h, v).wait()
        for k in range(1, peers):
            sixth(h, v, k).wait_recv()

    @pl.loop(0, 2)
    def _(v):
        for h in range(ROUNDS):
            fourth_local(h, v).wait()
            for k in range(1, peers):
                fourth(h, v, k).wait()

        @pl.loop(0, n)
        def _(src):
            for c in range(0, n, 2):
                both = [
                    jnp.concatenate(
                        [lines[:, :, v, src * n + c + p, part].reshape(nx, nz) for part in range(2)], axis=0
                    )
                    for p in range(2)
                ]
                weight = jnp.concatenate([screen[src, c], screen[src, c + 1]], axis=1)
                value = left(xf_ref, jnp.concatenate(both, axis=1))
                value = value * jnp.concatenate([weight, weight], axis=0)
                value = left(xi_ref, value)
                for p in range(2):
                    for part in range(2):
                        piece = value[part * nx:(part + 1) * nx, p * nz:(p + 1) * nz]
                        packed[:, :, v, src * n + c + p, part] = piece.reshape(ROUNDS, peers, n * PLANES, nz)

        sixth_start(0, v)

    def seventh(h, to):
        return remote(result.at[h, to], slab.at[h, z], s7.at[h, to], r7.at[h, z], band, line(to))

    def seventh_local(h, to):
        return pltpu.make_async_copy(result.at[h, to], slab.at[h, to], loc.at[6, h])

    def out_part(j, h):
        return out_ref.at[0, :, pl.ds(j * n + h * PLANES, PLANES)]

    def eighth(h, src):
        return remote(slab.at[h, src], out_part(band, h), s8.at[h, src], r8.at[h, band], PLANE_BAND[src], grid)

    def eighth_local(h, src):
        return pltpu.make_async_copy(slab.at[h, src], out_part(band, h), loc.at[7, h])

    def deliver(h):
        for src in range(n):
            @pl.when(z == src)
            def _():
                seventh_local(h, src).wait()

            @pl.when(z != src)
            def _():
                pltpu.make_async_remote_copy(
                    src_ref=result.at[h, src], dst_ref=slab.at[h, src],
                    send_sem=s7.at[h, src], recv_sem=r7.at[h, src],
                    device_id=(band, grid), device_id_type=pl.DeviceIdType.MESH,
                ).wait_recv()

            @pl.when(band == PLANE_BAND[src])
            def _():
                eighth_local(h, src).start()

            @pl.when(band != PLANE_BAND[src])
            def _():
                eighth(h, src).start()

    for h in range(ROUNDS):
        for v in range(2):
            sixth_wait(h, v)
            if h + 1 < ROUNDS:
                sixth_start(h + 1, v)
        for src in range(n):
            for p in range(PLANES):
                i = src * PLANES + p
                both = [
                    jnp.concatenate([back[h, :, v, :, part, i, :].reshape(ny, nz) for part in range(2)], axis=0)
                    for v in range(2)
                ]
                value = left(yi_ref, jnp.concatenate(both, axis=1))
                value = jnp.concatenate(
                    [
                        jnp.concatenate([value[:ny, v * nz:(v + 1) * nz], value[ny:, v * nz:(v + 1) * nz]], axis=1)
                        for v in range(2)
                    ],
                    axis=0,
                )
                value = -0.25 * right(value, zi_ref)
                total_re, total_im = 0.0, 0.0
                for v in range(2):
                    pot_re, pot_im = value[v * ny:(v + 1) * ny, :nz], value[v * ny:(v + 1) * ny, nz:]
                    vis_re, vis_im = held[h, src, v, 0, p], held[h, src, v, 1, p]
                    total_re = total_re + (pot_re * vis_re - pot_im * vis_im)
                    total_im = total_im + (pot_re * vis_im + pot_im * vis_re)
                result[h, src, 0, p] = total_re
                result[h, src, 1, p] = total_im

            @pl.when(z == src)
            def _():
                seventh_local(h, src).start()

            @pl.when(z != src)
            def _():
                seventh(h, src).start()
        if h > 1:
            deliver(h - 2)
    deliver(last - 1)
    deliver(last)

    for h in range(ROUNDS):
        for d in range(1, n):
            first(h, d).wait_send()
        for c in range(2):
            @pl.when(z != c + 1)
            def _():
                direct(h, c).wait_send()
        for v in range(2):
            for k in range(1, peers):
                sixth(h, v, k).wait_send()
        for src in range(n):
            @pl.when(z != src)
            def _():
                seventh(h, src).wait_send()

            @pl.when(band == PLANE_BAND[src])
            def _():
                eighth_local(h, src).wait()

            @pl.when(band != PLANE_BAND[src])
            def _():
                eighth(h, src).wait_send()

            @pl.when(band != src)
            def _():
                pltpu.make_async_remote_copy(
                    src_ref=slab.at[h, 0], dst_ref=out_part(src, h),
                    send_sem=s8.at[h, src], recv_sem=r8.at[h, src],
                    device_id=(band, grid), device_id_type=pl.DeviceIdType.MESH,
                ).wait_recv()
    for stream in range(ROUNDS + 1):
        hops_sent(stream, (0, 1, 2))


def fused(bands, coulomb):
    n = GROUPS
    spread = lax.axis_size("grid") // n
    peers = n * spread
    nx, ny, nz = coulomb.shape[0], bands.shape[3], bands.shape[4]
    rows = ny // peers
    q = np.arange(peers)
    row_order = (
        (np.arange(n)[None, :, None] * spread + (q % spread)[:, None, None]) * rows
        + (q // spread)[:, None, None] * n
        + np.arange(n)[None, None, :]
    ).reshape(-1)
    plane_order = (
        np.arange(n)[None, None, :, None] * (nx // n)
        + (q % spread)[None, :, None, None] * (nx // n // spread)
        + (q // spread)[None, :, None, None] * n
        + np.arange(ROUNDS)[:, None, None, None] * PLANES
        + np.arange(PLANES)
    ).reshape(-1)
    tabs = jnp.asarray(
        np.stack(permuted_tables(nx, 1.0 / (nx * ny * nz), row_order, plane_order)).astype(np.float32)
    )
    f32 = jnp.float32
    blocks = (ROUNDS, peers, 2, rows, 2, n * PLANES, nz)
    sem = pltpu.SemaphoreType.DMA
    return pl.pallas_call(
        functools.partial(fused_kernel, spread),
        in_specs=[pl.BlockSpec(memory_space=pltpu.HBM)] * 3,
        out_specs=pl.BlockSpec(memory_space=pl.ANY),
        out_shape=jax.ShapeDtypeStruct(bands.shape, f32),
        scratch_shapes=[
            pltpu.VMEM(tabs.shape, f32),
            pltpu.VMEM(tabs.shape[:1] + (2,) + tabs.shape[1:], jnp.bfloat16),
            pltpu.VMEM((nx, 2 * n, nz), f32),
            pltpu.VMEM((ROUNDS, n, n, 2, PLANES, ny, nz), f32),
            pltpu.VMEM((n, n, nx, nz), f32),
            pltpu.VMEM(blocks, f32),
            pltpu.VMEM(blocks, f32),
            pltpu.VMEM(blocks, f32),
            pltpu.VMEM((ROUNDS, n, 2, PLANES, ny, nz), f32),
            pltpu.VMEM((ROUNDS, n, 2, PLANES, ny, nz), f32),
            sem((ROUNDS, n)), sem((ROUNDS, n)),
            sem((ROUNDS, 2)), sem((ROUNDS, n)),
            sem((ROUNDS + 1, n)), sem((ROUNDS + 1, n)),
            sem((ROUNDS + 1, n)), sem((ROUNDS + 1, n)),
            sem((ROUNDS, 2, peers)), sem((ROUNDS, 2, peers)),
            sem((ROUNDS, 2, peers)), sem((ROUNDS, 2, peers)),
            sem((ROUNDS, n)), sem((ROUNDS, n)),
            sem((ROUNDS, n)), sem((ROUNDS, n)),
            sem((8, ROUNDS)),
        ],
        compiler_params=pltpu.CompilerParams(
            collective_id=0, has_side_effects=True, vmem_limit_bytes=VMEM_LIMIT
        ),
        name="exchange_by_planes",
    )(bands, coulomb, tabs)


def fits(bands, coulomb):
    groups, shards = lax.axis_size("band"), lax.axis_size("grid")
    return (
        bands.shape[0] == 1
        and groups == GROUPS
        and shards % GROUPS == 0
        and bands.shape[2] == GROUPS * GROUPS
        and bands.shape[3] == GROUPS * GROUPS * shards
        and coulomb.shape[0] == bands.shape[3] == bands.shape[4]
    )


def body(bands, coulomb):
    if fits(bands, coulomb):
        return fused(bands, coulomb)
    return by_pairs(bands, coulomb)


def solution(mesh):
    in_specs = (P("band", None, "grid", None, None), P(None, "grid", None))
    out_specs = P("band", None, "grid", None, None)
    return jax.shard_map(body, mesh=mesh, in_specs=in_specs, out_specs=out_specs, check_vma=False)
```
